256 devices in a mesh: group: 4 (over x), blk: 64 (over z, y, core).
Axes of the slice: x: 4, y: 4, z: 8, core: 2. Of those that a mesh axis runs over, the one named last changes fastest.
Arguments:
- features: bfloat16 [196608, 512], P(('group', 'blk')), may hold values from -6 to 6
- cotangent: bfloat16 [196608, 512], P(('group', 'blk')), may hold values from -6 to 6
- w_self: bfloat16 [512, 512], replicated, may hold values from -0.25 to 0.25
- w_neigh: bfloat16 [512, 512], replicated, may hold values from -0.25 to 0.25
- tile_src: int32 [256, 8, 2048], P(('group', 'blk')), may hold values from 0 to 767
- tile_dst: int32 [256, 8, 2048], P(('group', 'blk')), may hold values from 0 to 767
- tile_count: int32 [256, 8], P(('group', 'blk')), may hold values from 0 to 2048, as said below
- send_ids: int32 [256, 4, 256], P(('group', 'blk')), may hold values from 0 to 767
- recv_dst: int32 [256, 4, 256], P(('group', 'blk')), may hold values from 0 to 767
- recv_count: int32 [256, 4], P(('group', 'blk')), may hold values from 0 to 256, as said below
Outputs:
- grad_features: float32 [196608, 512], P(('group', 'blk'))
- grad_self: float32 [512, 512], replicated
- grad_neigh: float32 [512, 512], replicated
The draws below stay inside these ranges and needn't reach their ends.
Inputs may be any that keep to these rules, and one draw needn't show every extreme that they name: `tile_count`: some partition pair has exactly 2048 live slots; pairs differ in load, and some pairs have none. `recv_count`: some partition takes exactly 256 live slots from every group.
All inputs are finite; a program needn't handle non-finite values.
Results may differ from the reference program's by a relative error of at most 0.0027.
Values may be sent and summed in bfloat16 or wider, within the bound.
No kernel may reach another device: no remote copies, remote signals or barrier semaphores. Data moves between devices by JAX's collectives and lax.ppermute only.
A program may use at most 128 MiB of HBM per device.

```python
import math
import jax
import jax.numpy as jnp
from jax import lax

H = 512
NB = 768
OFFS = 8
EPT = 2048
CAP = 256
NDEV = 256
NODES = 196608
N_GROUP = 4
N_BLK = 64


def draw_tile_count(key, part):
    key = jax.random.fold_in(key, 11)
    keys = jax.random.split(key, 5)
    level = jax.random.randint(keys[0], (NDEV, 1), 1, 5)
    base = jax.random.randint(keys[1], (NDEV, OFFS), EPT // 8, EPT // 4 + 1)
    live = (jax.random.randint(keys[2], (NDEV, OFFS), 0, 4) > 0).astype(jnp.int32)
    counts = jnp.minimum(level * base, EPT) * live
    device = jax.random.randint(keys[3], (), 0, NDEV)
    offset = jax.random.randint(keys[4], (), 0, OFFS)
    counts = counts.at[device, offset].set(EPT)
    return counts.astype(jnp.int32)


def draw_recv_count(key, part):
    key = jax.random.fold_in(key, 23)
    keys = jax.random.split(key, 2)
    counts = jax.random.randint(keys[0], (NDEV, N_GROUP), 0, CAP + 1)
    device = jax.random.randint(keys[1], (), 0, NDEV)
    counts = counts.at[device].set(CAP)
    return counts.astype(jnp.int32)


def with_ends(entries, stream_key, smallest, largest):
    longest = entries.shape.index(max(entries.shape))
    spots = []
    for shift in (0, 1):
        where = [jax.random.randint(jax.random.fold_in(stream_key, axis), (), 0, length) for axis, length in enumerate(entries.shape)]
        where[longest] = (where[longest] + shift) % entries.shape[longest]
        spots.append(tuple(where))
    return entries.at[spots[0]].set(smallest).at[spots[1]].set(largest)


def shard_levels(rng, extent, cuts, least, top_value):
    def one(dim, blocks):
        steps = jax.random.uniform(jax.random.fold_in(jax.random.fold_in(rng, 6), dim), (blocks,), jnp.float32, least / len(cuts), top_value / len(cuts))
        return jnp.repeat(jnp.exp(steps), extent[dim] // blocks).reshape((-1,) + (1,) * (len(extent) - dim - 1))

    loudness = one(*cuts[0])
    for cut in cuts[1:]:
        loudness = loudness * one(*cut)
    return loudness


def noise(key, shape, spread, most, cuts=(), held_as=jnp.bfloat16):
    gain = shard_levels(key, shape, cuts, -0.22, 0.18) if cuts else 1.0
    result = jax.random.normal(key, shape, jnp.float32) * spread * gain
    return jnp.minimum(jnp.maximum(result, -most), most).astype(held_as)


def setup_inputs(seed: int = 0) -> dict:
    splits = jax.random.split(jax.random.key(seed), 11)
    return {
        "features": noise(splits[0], (NODES, H), 1.0, 6.0, ((0, 256),)),
        "cotangent": noise(splits[1], (NODES, H), 1.0, 6.0, ((0, 256),)),
        "w_self": noise(splits[2], (H, H), H ** -0.5, 0.25),
        "w_neigh": noise(splits[3], (H, H), H ** -0.5, 0.25),
        "tile_src": with_ends(jax.random.randint(splits[4], (NDEV, OFFS, EPT), 0, NB), jax.random.fold_in(splits[4], 1), 0, NB - 1).astype(jnp.int32),
        "tile_dst": with_ends(jax.random.randint(splits[5], (NDEV, OFFS, EPT), 0, NB), jax.random.fold_in(splits[5], 1), 0, NB - 1).astype(jnp.int32),
        "tile_count": draw_tile_count(jax.random.fold_in(splits[10], 71), 0),
        "send_ids": with_ends(jax.random.randint(splits[7], (NDEV, N_GROUP, CAP), 0, NB), jax.random.fold_in(splits[7], 1), 0, NB - 1).astype(jnp.int32),
        "recv_dst": with_ends(jax.random.randint(splits[8], (NDEV, N_GROUP, CAP), 0, NB), jax.random.fold_in(splits[8], 1), 0, NB - 1).astype(jnp.int32),
        "recv_count": draw_recv_count(jax.random.fold_in(splits[10], 71), 0),
    }


def reference(features, cotangent, w_self, w_neigh, tile_src, tile_dst, tile_count, send_ids, recv_dst, recv_count):
    feats = features.reshape(NDEV, NB, H)
    cots = cotangent.reshape(NDEV, NB, H)
    offsets = jnp.arange(OFFS, dtype=jnp.int32)
    groups = jnp.arange(N_GROUP, dtype=jnp.int32)
    slots = jnp.arange(EPT, dtype=jnp.int32)
    places = jnp.arange(CAP, dtype=jnp.int32)

    def forward(device):
        gidx = device // N_BLK
        bidx = device % N_BLK
        sources = (gidx * N_BLK + (bidx - offsets) % N_BLK).astype(jnp.int32)
        valid = (slots[None, :] < tile_count[device][:, None]).astype(jnp.float32)
        dst = tile_dst[device].reshape(-1)
        rows = feats[sources[:, None], tile_src[device]].astype(jnp.float32) * valid[:, :, None]
        summed = jax.ops.segment_sum(rows.reshape(-1, H), dst, num_segments=NB)
        peers = (groups * N_BLK + bidx).astype(jnp.int32)
        ids = send_ids[peers, gidx]
        bvalid = (places[None, :] < recv_count[device][:, None]).astype(jnp.float32)
        brows = feats[peers[:, None], ids].astype(jnp.float32) * bvalid[:, :, None]
        bdst = recv_dst[device].reshape(-1)
        summed = summed + jax.ops.segment_sum(brows.reshape(-1, H), bdst, num_segments=NB)
        degree = jax.ops.segment_sum(valid.reshape(-1), dst, num_segments=NB)
        degree = degree + jax.ops.segment_sum(bvalid.reshape(-1), bdst, num_segments=NB)
        inverse = 1.0 / jnp.maximum(degree, 1.0)
        aggregated = (inverse[:, None] * summed).astype(jnp.bfloat16)
        neigh = jnp.dot(cots[device], w_neigh.T, preferred_element_type=jnp.float32)
        scaled = (inverse[:, None] * neigh).astype(jnp.bfloat16)
        return (aggregated, scaled)
    aggregated, scaled = lax.map(forward, jnp.arange(NDEV, dtype=jnp.int32))

    def backward(device):
        gidx = device // N_BLK
        bidx = device % N_BLK
        senders = (gidx * N_BLK + (bidx + offsets) % N_BLK).astype(jnp.int32)
        counts = tile_count[senders, offsets]
        valid = (slots[None, :] < counts[:, None]).astype(jnp.float32)
        src = tile_src[senders, offsets]
        dst = tile_dst[senders, offsets]
        rows = scaled[senders[:, None], dst].astype(jnp.float32) * valid[:, :, None]
        total = jax.ops.segment_sum(rows.reshape(-1, H), src.reshape(-1), num_segments=NB)
        peers = (groups * N_BLK + bidx).astype(jnp.int32)
        bdst = recv_dst[peers, gidx]
        bvalid = (places[None, :] < recv_count[peers, gidx][:, None]).astype(jnp.float32)
        back = scaled[peers[:, None], bdst].astype(jnp.float32) * bvalid[:, :, None]
        total = total + jax.ops.segment_sum(back.reshape(-1, H), send_ids[device].reshape(-1), num_segments=NB)
        return total + jnp.dot(cots[device], w_self.T, preferred_element_type=jnp.float32)
    grad_features = lax.map(backward, jnp.arange(NDEV, dtype=jnp.int32)).reshape(NODES, H)
    factor = 1.0 / math.sqrt(NODES)
    grad_self = jnp.dot(features.T, cotangent, preferred_element_type=jnp.float32) * factor
    grad_neigh = jnp.dot(aggregated.reshape(NODES, H).T, cotangent, preferred_element_type=jnp.float32) * factor
    return (grad_features, grad_self, grad_neigh)
```

```python
import math

import jax
import jax.numpy as jnp
from jax import lax
from jax.experimental import pallas as pl
from jax.experimental.pallas import tpu as pltpu
from jax.sharding import PartitionSpec as P

F32 = jnp.float32
BF16 = jnp.bfloat16
I32 = jnp.int32
CHUNK = 1024
ALONG = (((1,), (1,)), ((), ()))
DOWN = (((0,), (0,)), ((), ()))


def dot(a, b, dims=(((1,), (0,)), ((), ()))):
    return lax.dot_general(a, b, dims, preferred_element_type=F32)


def hot(rows, ids):
    spots = lax.broadcasted_iota(I32, (rows, ids.shape[1]), 0)
    return jnp.where(spots == ids, 1.0, 0.0).astype(BF16)


def small_hot(rows, ids):
    spots = lax.broadcasted_iota(jnp.int16, (rows, ids.shape[1]), 0)
    ones = jnp.where(spots == ids.astype(jnp.int16), jnp.ones((), BF16), jnp.zeros((), BF16))
    return ones.astype(jnp.float8_e4m3fn)


def prepare(tcount, rcount, tdst, rdst, rcol, cot, x_out, rows_out):
    nodes = cot.shape[0]
    offs, ept = tdst.shape[1], tdst.shape[2]
    ngroup, cap = rdst.shape[1], rdst.shape[2]
    counts = jnp.zeros((32, 32), F32)

    def tally(ids, live):
        ids = jnp.where(lax.broadcasted_iota(I32, ids.shape, 1) < live, ids, 1023)
        return dot(hot(32, ids >> 5), hot(32, ids & 31), ALONG)

    for s in range(offs):
        counts = counts + tally(tdst[0, s : s + 1, :], tcount[0, s])
    for g in range(ngroup):
        counts = counts + tally(rdst[0, g : g + 1, :], rcount[0, g])
    upper = jnp.floor(counts * (1.0 / 128.0))
    lower = counts - upper * 128.0
    node = lax.broadcasted_iota(I32, (nodes, 32), 0)
    lane = lax.broadcasted_iota(I32, (nodes, 32), 1)
    pick = jnp.where((node >> 5) == lane, 1.0, 0.0).astype(BF16)
    spread = dot(pick, upper.astype(BF16)) * 128.0 + dot(pick, lower.astype(BF16))
    degree = jnp.sum(jnp.where((node & 31) == lane, spread, 0.0), axis=1, keepdims=True)
    inverse = 1.0 / jnp.maximum(degree, 1.0)
    x = (inverse * cot[...].astype(F32)).astype(BF16)
    x_out[...] = x
    slot = lax.broadcasted_iota(I32, (cap, 1), 0)
    along = lax.broadcasted_iota(I32, (cap, nodes), 1)
    for g in range(ngroup):
        ids = jnp.where(slot < rcount[0, g], rcol[:, g : g + 1], -1)
        pickrow = jnp.where(along == ids, 1.0, 0.0).astype(BF16)
        rows_out[g] = dot(pickrow, x).astype(BF16)


def build(chunks, edges, tile_out, acc):
    s = pl.program_id(0)
    nodes = acc.shape[0]
    acc[...] = jnp.zeros_like(acc)

    def step(i, carry):
        packed = edges[0, :, pl.ds(pl.multiple_of(i * CHUNK, CHUNK), CHUNK)]
        acc[...] += dot(small_hot(nodes, packed >> 10), small_hot(nodes, packed & 1023), ALONG)
        return carry

    lax.fori_loop(0, chunks[s], step, 0)
    tile_out[0] = acc[...].astype(BF16)


def first_sum(tile0, tile1, x0, x1, ids, rows, out):
    i = pl.program_id(0)
    block = out.shape[0]
    total = dot(tile0[0], x0[...]) + dot(tile1[0], x1[...])
    spots = lax.broadcasted_iota(I32, (block, ids.shape[1]), 0) + i * block
    sel = jnp.where(spots == ids[...], 1.0, 0.0).astype(BF16)
    out[...] = total + dot(sel, rows[...])


def middle_sum(before, t0, t1, t2, t3, x0, x1, x2, x3, out):
    total = before[...] + dot(t0[0], x0[...]) + dot(t1[0], x1[...])
    out[...] = total + dot(t2[0], x2[...]) + dot(t3[0], x3[...])


def last_sum(before, t0, t1, x0, x1, feats, out, grad):
    i = pl.program_id(0)
    total = before[...] + dot(t0[0], x0[...]) + dot(t1[0], x1[...])
    out[...] = total
    top = total.astype(BF16)
    rest = (total - top.astype(F32)).astype(BF16)
    part = dot(feats[...], top, DOWN) + dot(feats[...], rest, DOWN)

    @pl.when(i == 0)
    def _():
        grad[...] = part

    @pl.when(i > 0)
    def _():
        grad[...] += part


def finish(summed, cot, w_self, w_neigh, out):
    total = summed[...]
    top = total.astype(BF16)
    rest = (total - top.astype(F32)).astype(BF16)
    out[...] = (
        dot(cot[...], w_self[...], ALONG)
        + dot(top, w_neigh[...], ALONG)
        + dot(rest, w_neigh[...], ALONG)
    )


BLOCK = 256
LIMIT = 40 * 1024 * 1024


def params():
    return pltpu.CompilerParams(vmem_limit_bytes=LIMIT)


def whole(shape):
    return pl.BlockSpec(shape, lambda i: (0,) * len(shape))


def tile_spec(slot, nodes):
    return pl.BlockSpec((1, BLOCK, nodes), lambda i: (slot, i, 0))


def row_spec(width):
    return pl.BlockSpec((BLOCK, width), lambda i: (i, 0))


def estimate(macs, moved):
    return pl.CostEstimate(flops=2 * macs, bytes_accessed=moved, transcendentals=0)


def run_prepare(tile_count, recv_count, tile_dst, recv_dst, recv_col, cotangent):
    nodes, width = cotangent.shape
    ngroup, cap = recv_dst.shape[1], recv_dst.shape[2]
    vm = pl.BlockSpec(memory_space=pltpu.VMEM)
    sm = pl.BlockSpec(memory_space=pltpu.SMEM)
    return pl.pallas_call(
        prepare,
        out_shape=(
            jax.ShapeDtypeStruct((nodes, width), BF16),
            jax.ShapeDtypeStruct((ngroup, cap, width), BF16),
        ),
        in_specs=[sm, sm, vm, vm, vm, vm],
        out_specs=(vm, vm),
        compiler_params=params(),
        cost_estimate=estimate(ngroup * cap * nodes * width, 4 * nodes * width),
        name="prepare",
    )(tile_count, recv_count, tile_dst, recv_dst, recv_col, cotangent)


def run_build(chunks, edges, nodes):
    slots, _, ept = edges.shape
    return pl.pallas_call(
        build,
        grid_spec=pltpu.PrefetchScalarGridSpec(
            num_scalar_prefetch=1,
            grid=(slots,),
            in_specs=[pl.BlockSpec((1, 1, ept), lambda s, c: (s, 0, 0))],
            out_specs=pl.BlockSpec((1, nodes, nodes), lambda s, c: (s, 0, 0)),
            scratch_shapes=[pltpu.VMEM((nodes, nodes), F32)],
        ),
        out_shape=jax.ShapeDtypeStruct((slots, nodes, nodes), BF16),
        compiler_params=params(),
        cost_estimate=estimate(slots * nodes * nodes * ept, 2 * slots * nodes * nodes),
        name="build",
    )(chunks, edges)


def run_first(tiles, x0, x1, ids, rows):
    nodes, width = x0.shape
    return pl.pallas_call(
        first_sum,
        grid=(nodes // BLOCK,),
        in_specs=[
            tile_spec(0, nodes),
            tile_spec(1, nodes),
            whole(x0.shape),
            whole(x1.shape),
            whole(ids.shape),
            whole(rows.shape),
        ],
        out_specs=row_spec(width),
        out_shape=jax.ShapeDtypeStruct((nodes, width), F32),
        compiler_params=params(),
        cost_estimate=estimate(3 * nodes * nodes * width, 12 * nodes * width),
        name="first_sum",
    )(tiles, tiles, x0, x1, ids, rows)


def run_middle(before, tiles, slots, xs):
    nodes, width = before.shape
    return pl.pallas_call(
        middle_sum,
        grid=(nodes // BLOCK,),
        in_specs=[row_spec(width)]
        + [tile_spec(s, nodes) for s in slots]
        + [whole(x.shape) for x in xs],
        out_specs=row_spec(width),
        out_shape=jax.ShapeDtypeStruct((nodes, width), F32),
        compiler_params=params(),
        cost_estimate=estimate(4 * nodes * nodes * width, 16 * nodes * width),
        name="middle_sum",
    )(before, *([tiles] * len(slots)), *xs)


def run_last(before, tiles, slots, xs, features):
    nodes, width = before.shape
    return pl.pallas_call(
        last_sum,
        grid=(nodes // BLOCK,),
        in_specs=[row_spec(width)]
        + [tile_spec(s, nodes) for s in slots]
        + [whole(x.shape) for x in xs]
        + [row_spec(width)],
        out_specs=(row_spec(width), whole((width, width))),
        out_shape=(
            jax.ShapeDtypeStruct((nodes, width), F32),
            jax.ShapeDtypeStruct((width, width), F32),
        ),
        compiler_params=params(),
        cost_estimate=estimate(3 * nodes * nodes * width, 16 * nodes * width),
        name="last_sum",
    )(before, *([tiles] * len(slots)), *xs, features)


def run_finish(summed, cotangent, w_self, w_neigh):
    nodes, width = summed.shape
    return pl.pallas_call(
        finish,
        grid=(nodes // BLOCK,),
        in_specs=[row_spec(width), row_spec(width), whole(w_self.shape), whole(w_neigh.shape)],
        out_specs=row_spec(width),
        out_shape=jax.ShapeDtypeStruct((nodes, width), F32),
        compiler_params=params(),
        cost_estimate=estimate(3 * nodes * width * width, 10 * nodes * width),
        name="finish",
    )(summed, cotangent, w_self, w_neigh)


def moved(value, perm):
    return lax.ppermute(value, "blk", perm)


def pick_piece(pieces, index):
    out = pieces[0]
    for k in range(1, len(pieces)):
        out = jnp.where(index == k, pieces[k], out)
    return out


def scatter_sum(value, index, count, send):
    size = value.shape[0] // count
    pieces = [value[k * size : (k + 1) * size] for k in range(count)]
    total = pick_piece(pieces, index)
    for s in range(1, count):
        total = total + send(pick_piece(pieces, (index + s) % count), s)
    return total


def gather_all(piece, index, count, send):
    held = [piece] + [send(piece, s) for s in range(1, count)]
    return jnp.concatenate(
        [pick_piece(held, (index - k) % count) for k in range(count)], axis=0
    )


def on_device(
    features,
    cotangent,
    w_self,
    w_neigh,
    tile_src,
    tile_dst,
    tile_count,
    send_ids,
    recv_dst,
    recv_count,
):
    nodes, width = features.shape
    offs, ept = tile_src.shape[1], tile_src.shape[2]
    ngroup, cap = send_ids.shape[1], send_ids.shape[2]
    nblk = lax.axis_size("blk")
    gi = lax.axis_index("group")
    bi = lax.axis_index("blk")
    core = bi % 2
    ypos = (bi // 2) % 4
    ring = range(nblk)
    swap = [(i, i ^ 1) for i in ring]

    def yshift(by):
        return [(i, (i // 8) * 8 + (i % 8 + 2 * by) % 8) for i in ring]

    def zflip(k):
        return [(i, (i // 8 ^ k) * 8 + i % 8) for i in ring]

    live = lax.broadcasted_iota(I32, (offs, ept), 1) < tile_count[0][:, None]
    lists = jnp.where(live, tile_src[0] * 1024 + tile_dst[0], -1)[:, None, :]
    mine = [lists[s] for s in range(offs)]
    slots = [None] * offs
    slots[0] = mine[0]
    slots[1] = moved(
        jnp.where(core == 1, mine[1], mine[7]),
        [(i, (i - 1 if i % 2 else i - 7) % nblk) for i in ring],
    )
    for j in (1, 2, 3):
        slots[2 * j] = moved(mine[2 * j], [(i, (i - 2 * j) % nblk) for i in ring])
        slots[2 * j + 1] = moved(
            jnp.where(core == 1, mine[2 * j + 1], mine[2 * j - 1]),
            [(i, (i - 2 * j + 1 - 2 * (i % 2)) % nblk) for i in ring],
        )
    edges = jnp.stack(slots)
    chunks = jnp.sum((edges[:, 0, ::CHUNK] >= 0).astype(I32), axis=1)

    x, rows = run_prepare(
        tile_count, recv_count, tile_dst, recv_dst, recv_dst[0].T, cotangent
    )
    returned = lax.all_to_all(rows, "group", split_axis=0, concat_axis=0, tiled=True)
    far = moved(x, [(i, (i - 8) % nblk) for i in ring])
    one = moved(jnp.where(ypos == 0, far, x), yshift(-1))
    three = moved(jnp.where(ypos == 3, x, far), yshift(1))
    side = moved(jnp.where(core == 1, x, far), swap)
    two = moved(
        jnp.where(core == 0, one, three),
        [(i, (i - 2 if i % 2 == 0 else i + 2) % nblk) for i in ring],
    )
    one_b = moved(one, swap)
    three_b = moved(three, swap)
    two_b = moved(two, swap)

    tiles = run_build(chunks, edges, nodes)
    summed = run_first(
        tiles, x, side, send_ids.reshape(1, ngroup * cap), returned.reshape(ngroup * cap, width)
    )
    summed = run_middle(summed, tiles, (2, 3, 6, 7), (one, one_b, three, three_b))
    summed, neigh_part = run_last(summed, tiles, (4, 5), (two, two_b), features)
    total = run_finish(summed, cotangent, w_self, w_neigh)
    self_part = dot(features, cotangent, DOWN)

    grads = jnp.stack([self_part, neigh_part]).reshape(2, width, width)
    grads = grads.transpose(1, 0, 2)

    def over_core(v, s):
        return moved(v, swap)

    def over_group(v, s):
        return lax.ppermute(v, "group", [(i, (i + s) % ngroup) for i in range(ngroup)])

    def over_y(v, s):
        return moved(v, yshift(s))

    grads = scatter_sum(grads, core, 2, over_core)
    grads = scatter_sum(grads, gi, ngroup, over_group)
    grads = scatter_sum(grads, ypos, 4, over_y)
    for k in (1, 2, 4):
        grads = grads + moved(grads, zflip(k))
    grads = gather_all(grads, ypos, 4, over_y)
    grads = gather_all(grads, gi, ngroup, over_group)
    grads = gather_all(grads, core, 2, over_core)
    factor = 1.0 / math.sqrt(nodes * lax.axis_size("group") * nblk)
    return (total, grads[:, 0] * factor, grads[:, 1] * factor)


def solution(mesh):
    both = ("group", "blk")
    placed = (
        P(both, None),
        P(both, None),
        P(),
        P(),
        P(both, None, None),
        P(both, None, None),
        P(both, None),
        P(both, None, None),
        P(both, None, None),
        P(both, None),
    )
    return jax.shard_map(
        on_device,
        mesh=mesh,
        in_specs=placed,
        out_specs=(P(both, None), P(), P()),
        check_vma=False,
    )
```

```python
import math

import jax
import jax.numpy as jnp
from jax import lax
from jax.experimental import pallas as pl
from jax.experimental.pallas import tpu as pltpu
from jax.sharding import PartitionSpec as P

F32 = jnp.float32
BF16 = jnp.bfloat16
I32 = jnp.int32
CHUNK = 1024
ALONG = (((1,), (1,)), ((), ()))
DOWN = (((0,), (0,)), ((), ()))


def dot(a, b, dims=(((1,), (0,)), ((), ()))):
    return lax.dot_general(a, b, dims, preferred_element_type=F32)


def hot(rows, ids):
    spots = lax.broadcasted_iota(I32, (rows, ids.shape[1]), 0)
    return jnp.where(spots == ids, 1.0, 0.0).astype(BF16)


def small_hot(rows, ids):
    spots = lax.broadcasted_iota(jnp.int16, (rows, ids.shape[1]), 0)
    ones = jnp.where(spots == ids.astype(jnp.int16), jnp.ones((), BF16), jnp.zeros((), BF16))
    return ones.astype(jnp.float8_e4m3fn)


def prepare(tcount, rcount, tsrc, tdst, rdst, cot, x_out, rows_out, own, first, pair1, pair2, pair3):
    nodes = cot.shape[0]
    offs, ept = tdst.shape[1], tdst.shape[2]
    ngroup, cap = rdst.shape[1], rdst.shape[2]
    odd = lax.rem(lax.axis_index("blk"), 2) == 1
    slot = lax.broadcasted_iota(I32, (1, ept), 1)
    counts = jnp.zeros((32, 32), F32)
    lists = []
    for s in range(offs):
        live = slot < tcount[0:1, s : s + 1]
        ids = jnp.where(live, tdst[0, s : s + 1, :], 1023)
        counts = counts + dot(hot(32, ids >> 5), hot(32, ids & 31), ALONG)
        lists.append(jnp.where(live, tsrc[0, s : s + 1, :] * 1024 + ids, -1))
    own[...] = lists[0]
    first[...] = jnp.where(odd, lists[1], lists[7])
    for j, pair in ((1, pair1), (2, pair2), (3, pair3)):
        pair[0:1, :] = lists[2 * j]
        pair[1:2, :] = jnp.where(odd, lists[2 * j + 1], lists[2 * j - 1])
    slot = lax.broadcasted_iota(I32, (1, cap), 1)
    marked = []
    for g in range(ngroup):
        ids = jnp.where(slot < rcount[0:1, g : g + 1], rdst[0, g : g + 1, :], 1023)
        counts = counts + dot(hot(32, ids >> 5), hot(32, ids & 31), ALONG)
        marked.append(hot(nodes, ids))
    upper = jnp.floor(counts * (1.0 / 128.0))
    lower = counts - upper * 128.0
    node = lax.broadcasted_iota(I32, (nodes, 32), 0)
    lane = lax.broadcasted_iota(I32, (nodes, 32), 1)
    pick = jnp.where((node >> 5) == lane, 1.0, 0.0).astype(BF16)
    spread = dot(pick, upper.astype(BF16)) * 128.0 + dot(pick, lower.astype(BF16))
    degree = jnp.sum(jnp.where((node & 31) == lane, spread, 0.0), axis=1, keepdims=True)
    inverse = 1.0 / jnp.maximum(degree, 1.0)
    x = (inverse * cot[...].astype(F32)).astype(BF16)
    x_out[...] = x
    for g in range(ngroup):
        rows_out[g] = dot(marked[g], x, DOWN).astype(BF16)


def build(edges, tile_out, acc):
    nodes = acc.shape[0]
    acc[...] = jnp.zeros_like(acc)
    live = jnp.sum((edges[0] >= 0).astype(I32))

    def step(i, carry):
        packed = edges[0, :, pl.ds(pl.multiple_of(i * CHUNK, CHUNK), CHUNK)]
        acc[...] += dot(small_hot(nodes, packed >> 10), small_hot(nodes, packed & 1023), ALONG)
        return carry

    lax.fori_loop(0, (live + CHUNK - 1) // CHUNK, step, 0)
    tile_out[0] = acc[...].astype(BF16)


def first_sum(tile0, tile1, x0, x1, ids, rows, out):
    i = pl.program_id(0)
    block = out.shape[0]
    total = dot(tile0[0], x0[...]) + dot(tile1[0], x1[...])
    spots = lax.broadcasted_iota(I32, (block, ids.shape[1]), 0) + i * block
    sel = jnp.where(spots == ids[...], 1.0, 0.0).astype(BF16)
    out[...] = total + dot(sel, rows[...])


def middle_sum(before, t0, t1, t2, t3, x0, x1, x2, x3, out):
    total = before[...] + dot(t0[0], x0[...]) + dot(t1[0], x1[...])
    out[...] = total + dot(t2[0], x2[...]) + dot(t3[0], x3[...])


def last_sum(before, t0, t1, x0, x1, feats, out, send, keep, grad):
    nodes = before.shape[0]
    for i in range(nodes // BLOCK):
        rows = slice(i * BLOCK, (i + 1) * BLOCK)
        total = before[rows, :] + dot(t0[0, rows, :], x0[...]) + dot(t1[0, rows, :], x1[...])
        out[rows, :] = total
        top = total.astype(BF16)
        rest = (total - top.astype(F32)).astype(BF16)
        part = dot(feats[rows, :], top, DOWN) + dot(feats[rows, :], rest, DOWN)
        if i == 0:
            grad[...] = part
        else:
            grad[...] += part
    half = send.shape[0]
    core = lax.rem(lax.axis_index("blk"), 2)
    keep[...] = grad[pl.ds(pl.multiple_of(core * half, half), half), :]
    send[...] = grad[pl.ds(pl.multiple_of((1 - core) * half, half), half), :]


def place(factor, *refs):
    out_self, out_neigh = refs[-2], refs[-1]
    ngroup = (len(refs) - 2) // 2
    size = refs[0].shape[1]
    group, core = lax.axis_index("group"), lax.rem(lax.axis_index("blk"), 2)
    for n in range(2 * ngroup):
        k = core if n < ngroup else 1 - core
        g = lax.rem(group - n % ngroup + ngroup, ngroup)
        at = pl.multiple_of((k * ngroup + g) * size, size)
        out_self[pl.ds(at, size), :] = refs[n][0] * factor
        out_neigh[pl.ds(at, size), :] = refs[n][1] * factor


def finish(summed, cot, w_self, w_neigh, out):
    total = summed[...]
    top = total.astype(BF16)
    rest = (total - top.astype(F32)).astype(BF16)
    out[...] = (
        dot(cot[...], w_self[...], ALONG)
        + dot(top, w_neigh[...], ALONG)
        + dot(rest, w_neigh[...], ALONG)
    )


BLOCK = 256
MIB = 1024 * 1024


def params(mib):
    return pltpu.CompilerParams(vmem_limit_bytes=mib * MIB)


def whole(shape):
    return pl.BlockSpec(shape, lambda i: (0,) * len(shape))


def tile_spec(slot, nodes):
    return pl.BlockSpec((1, BLOCK, nodes), lambda i: (slot, i, 0))


def row_spec(width):
    return pl.BlockSpec((BLOCK, width), lambda i: (i, 0))


def estimate(macs, moved):
    return pl.CostEstimate(flops=2 * macs, bytes_accessed=moved, transcendentals=0)


def run_prepare(tile_count, recv_count, tile_src, tile_dst, recv_dst, cotangent):
    nodes, width = cotangent.shape
    ngroup, cap = recv_dst.shape[1], recv_dst.shape[2]
    ept = tile_src.shape[2]
    given = (tile_count, recv_count, tile_src, tile_dst, recv_dst, cotangent)
    made = [((nodes, width), BF16), ((ngroup, cap, width), BF16)]
    made += [((1, ept), I32)] * 2 + [((2, ept), I32)] * 3
    return pl.pallas_call(
        prepare,
        grid=(1,),
        out_shape=[jax.ShapeDtypeStruct(*m) for m in made],
        in_specs=[whole(v.shape) for v in given],
        out_specs=[whole(m[0]) for m in made],
        compiler_params=params(60),
        cost_estimate=estimate(ngroup * cap * nodes * width, 4 * nodes * width),
        name="prepare",
    )(*given)


def run_build(edges, nodes):
    slots, _, ept = edges.shape
    return pl.pallas_call(
        build,
        grid=(slots,),
        in_specs=[pl.BlockSpec((1, 1, ept), lambda s: (s, 0, 0))],
        out_specs=pl.BlockSpec((1, nodes, nodes), lambda s: (s, 0, 0)),
        scratch_shapes=[pltpu.VMEM((nodes, nodes), F32)],
        out_shape=jax.ShapeDtypeStruct((slots, nodes, nodes), BF16),
        compiler_params=params(24),
        cost_estimate=estimate(slots * nodes * nodes * ept // 2, 2 * slots * nodes * nodes),
        name="build",
    )(edges)


def run_first(tiles, x0, x1, ids, rows):
    nodes, width = x0.shape
    return pl.pallas_call(
        first_sum,
        grid=(nodes // BLOCK,),
        in_specs=[
            tile_spec(0, nodes),
            tile_spec(1, nodes),
            whole(x0.shape),
            whole(x1.shape),
            whole(ids.shape),
            whole(rows.shape),
        ],
        out_specs=row_spec(width),
        out_shape=jax.ShapeDtypeStruct((nodes, width), F32),
        compiler_params=params(24),
        cost_estimate=estimate(3 * nodes * nodes * width, 12 * nodes * width),
        name="first_sum",
    )(tiles, tiles, x0, x1, ids, rows)


def run_middle(before, own, other, xs):
    nodes, width = before.shape
    return pl.pallas_call(
        middle_sum,
        grid=(nodes // BLOCK,),
        in_specs=[row_spec(width)]
        + [tile_spec(s, nodes) for s in (0, 1, 0, 1)]
        + [whole(x.shape) for x in xs],
        out_specs=row_spec(width),
        out_shape=jax.ShapeDtypeStruct((nodes, width), F32),
        compiler_params=params(24),
        cost_estimate=estimate(4 * nodes * nodes * width, 16 * nodes * width),
        name="middle_sum",
    )(before, own, own, other, other, *xs)


def run_last(before, own, other, xs, features):
    nodes, width = before.shape
    vm = pl.BlockSpec(memory_space=pltpu.VMEM)
    return pl.pallas_call(
        last_sum,
        in_specs=[vm] * 6,
        out_specs=[vm] * 3,
        out_shape=(
            jax.ShapeDtypeStruct((nodes, width), F32),
            jax.ShapeDtypeStruct((width // 2, width), F32),
            jax.ShapeDtypeStruct((width // 2, width), F32),
        ),
        scratch_shapes=[pltpu.VMEM((width, width), F32)],
        compiler_params=params(24),
        cost_estimate=estimate(3 * nodes * nodes * width, 16 * nodes * width),
        name="last_sum",
    )(before, own, other, *xs, features)


def run_place(pieces, factor, width):
    return pl.pallas_call(
        lambda *refs: place(factor, *refs),
        grid=(1,),
        in_specs=[whole(v.shape) for v in pieces],
        out_specs=[whole((width, width))] * 2,
        out_shape=[jax.ShapeDtypeStruct((width, width), F32)] * 2,
        compiler_params=params(24),
        cost_estimate=estimate(width * width, 16 * width * width),
        name="place",
    )(*pieces)


def run_finish(summed, cotangent, w_self, w_neigh):
    nodes, width = summed.shape
    return pl.pallas_call(
        finish,
        grid=(nodes // BLOCK,),
        in_specs=[row_spec(width), row_spec(width), whole(w_self.shape), whole(w_neigh.shape)],
        out_specs=row_spec(width),
        out_shape=jax.ShapeDtypeStruct((nodes, width), F32),
        compiler_params=params(24),
        cost_estimate=estimate(3 * nodes * width * width, 10 * nodes * width),
        name="finish",
    )(summed, cotangent, w_self, w_neigh)


def moved(value, perm):
    return lax.ppermute(value, "blk", perm)


def over_group(value):
    return lax.all_to_all(value, "group", split_axis=0, concat_axis=0, tiled=True)


def fence(values):
    return lax.optimization_barrier(values)


def on_device(
    features,
    cotangent,
    w_self,
    w_neigh,
    tile_src,
    tile_dst,
    tile_count,
    send_ids,
    recv_dst,
    recv_count,
):
    nodes, width = features.shape
    ngroup, cap = send_ids.shape[1], send_ids.shape[2]
    ny = 4
    nblk = lax.axis_size("blk")
    bi = lax.axis_index("blk")
    core = bi % 2
    ypos = (bi // 2) % ny
    ring = range(nblk)
    swap = [(i, i ^ 1) for i in ring]

    def yshift(by):
        return [(i, (i // 8) * 8 + (i % 8 + 2 * by) % 8) for i in ring]

    x, rows, own, first, pair1, pair2, pair3 = run_prepare(
        tile_count, recv_count, tile_src, tile_dst, recv_dst, cotangent
    )
    far = moved(x, [(i, (i - 8) % nblk) for i in ring])
    first = moved(first, [(i, (i - 1 if i % 2 else i - 7) % nblk) for i in ring])
    pairs = [
        moved(p, [(i, (i - 2 * j) % nblk) for i in ring])
        for j, p in ((1, pair1), (2, pair2), (3, pair3))
    ]
    self_part = dot(features, cotangent, DOWN)
    near = run_build(jnp.stack([own, first]), nodes)
    mine = run_build(jnp.stack([pairs[0][0:1], pairs[2][0:1]]), nodes)
    x, far, rows = fence((x, far, rows, near, mine, self_part))[:3]

    one = moved(jnp.where(ypos == 0, far, x), yshift(-1))
    three = moved(jnp.where(ypos == 3, x, far), yshift(1))
    other = moved(jnp.concatenate([p[1:2] for p in pairs], axis=0), swap)
    side = moved(jnp.where(core == 1, x, far), swap)
    returned = lax.all_to_all(rows, "group", split_axis=0, concat_axis=0, tiled=True)
    theirs = run_build(jnp.stack([other[0:1], other[2:3]]), nodes)
    mid_own = run_build(pairs[1][None, 0:1], nodes)
    mid_other = run_build(other[None, 1:2], nodes)
    summed = run_first(
        near, x, side, send_ids.reshape(1, ngroup * cap), returned.reshape(ngroup * cap, width)
    )
    one, three = fence((one, three, theirs, mid_own, mid_other, summed))[:2]

    two = moved(
        jnp.where(core == 0, one, three),
        [(i, (i - 2 if i % 2 == 0 else i + 2) % nblk) for i in ring],
    )
    one_b = moved(one, swap)
    three_b = moved(three, swap)
    half = width // 2
    self_part = jnp.where(core == 0, self_part[:half], self_part[half:]) + moved(
        jnp.where(core == 0, self_part[half:], self_part[:half]), swap
    )
    self_part = over_group(self_part.reshape(ngroup, half // ngroup, width)).sum(0)
    summed = run_middle(summed, mine, theirs, (one, three, one_b, three_b))
    two = fence((two, summed, self_part))[0]

    two_b = moved(two, swap)
    summed, send, keep = run_last(summed, mid_own, mid_other, (two, two_b), features)

    part = keep + moved(send, swap)
    part = over_group(part.reshape(ngroup, half // ngroup, width)).sum(0)
    rest = nblk // 2
    size = half // ngroup // rest
    planes = [[2 * i + c for i in range(rest)] for c in range(2)]

    def over_plane(v):
        return lax.all_to_all(
            v, "blk", split_axis=0, concat_axis=0, tiled=True, axis_index_groups=planes
        )

    part = jnp.stack([self_part, part]).reshape(2, rest, size, width).transpose(1, 0, 2, 3)
    part = over_plane(part).sum(0)
    part = over_plane(jnp.broadcast_to(part[None], (rest, 2, size, width)))
    part = part.transpose(1, 0, 2, 3).reshape(2, rest * size, width)
    held = [part] + [
        lax.ppermute(part, "group", [(i, (i + s) % ngroup) for i in range(ngroup)])
        for s in range(1, ngroup)
    ]
    held = held + [moved(v, swap) for v in held]
    total = run_finish(summed, cotangent, w_self, w_neigh)
    factor = 1.0 / math.sqrt(nodes * lax.axis_size("group") * nblk)
    grad_self, grad_neigh = run_place(held, factor, width)
    return (total, grad_self, grad_neigh)


def solution(mesh):
    both = ("group", "blk")
    placed = (
        P(both, None),
        P(both, None),
        P(),
        P(),
        P(both, None, None),
        P(both, None, None),
        P(both, None),
        P(both, None, None),
        P(both, None, None),
        P(both, None),
    )
    return jax.shard_map(
        on_device,
        mesh=mesh,
        in_specs=placed,
        out_specs=(P(both, None), P(), P()),
        check_vma=False,
    )
```

```python
import math

import jax
import jax.numpy as jnp
from jax import lax
from jax.experimental import pallas as pl
from jax.experimental.pallas import tpu as pltpu
from jax.sharding import Mesh
from jax.sharding import PartitionSpec as P

F32 = jnp.float32
BF16 = jnp.bfloat16
I32 = jnp.int32
CHUNK = 1024
ALONG = (((1,), (1,)), ((), ()))
DOWN = (((0,), (0,)), ((), ()))


def dot(a, b, dims=(((1,), (0,)), ((), ()))):
    return lax.dot_general(a, b, dims, preferred_element_type=F32)


def hot(rows, ids):
    spots = lax.broadcasted_iota(I32, (rows, ids.shape[1]), 0)
    return jnp.where(spots == ids, 1.0, 0.0).astype(BF16)


def small_hot(rows, ids):
    spots = lax.broadcasted_iota(jnp.int16, (rows, ids.shape[1]), 0)
    ones = jnp.where(spots == ids.astype(jnp.int16), jnp.ones((), BF16), jnp.zeros((), BF16))
    return ones.astype(jnp.float8_e4m3fn)


def pack(tcount, tsrc, tdst, own, first, pair1, pair2, pair3):
    offs, ept = tdst.shape[1], tdst.shape[2]
    odd = lax.axis_index("core") == 1
    slot = lax.broadcasted_iota(I32, (1, ept), 1)

    def packed(s):
        live = slot < tcount[0:1, s : s + 1]
        return jnp.where(live, tsrc[0, s : s + 1, :] * 1024 + tdst[0, s : s + 1, :], -1)

    lists = [packed(s) for s in range(offs)]
    own[...] = lists[0]
    first[...] = jnp.where(odd, lists[1], lists[7])
    for j, pair in ((1, pair1), (2, pair2), (3, pair3)):
        pair[0:1, :] = lists[2 * j]
        pair[1:2, :] = jnp.where(odd, lists[2 * j + 1], lists[2 * j - 1])


def prepare(tcount, rcount, tdst, rdst, cot, x_out, rows_out):
    nodes = cot.shape[0]
    offs, ept = tdst.shape[1], tdst.shape[2]
    ngroup, cap = rdst.shape[1], rdst.shape[2]
    slot = lax.broadcasted_iota(I32, (1, ept), 1)
    counts = jnp.zeros((32, 32), F32)
    for s in range(offs):
        ids = jnp.where(slot < tcount[0:1, s : s + 1], tdst[0, s : s + 1, :], 1023)
        counts = counts + dot(hot(32, ids >> 5), hot(32, ids & 31), ALONG)
    slot = lax.broadcasted_iota(I32, (1, cap), 1)
    marked = []
    for g in range(ngroup):
        ids = jnp.where(slot < rcount[0:1, g : g + 1], rdst[0, g : g + 1, :], 1023)
        counts = counts + dot(hot(32, ids >> 5), hot(32, ids & 31), ALONG)
        marked.append(hot(nodes, ids))
    upper = jnp.floor(counts * (1.0 / 128.0))
    lower = counts - upper * 128.0
    node = lax.broadcasted_iota(I32, (nodes, 32), 0)
    lane = lax.broadcasted_iota(I32, (nodes, 32), 1)
    pick = jnp.where((node >> 5) == lane, 1.0, 0.0).astype(BF16)
    spread = dot(pick, upper.astype(BF16)) * 128.0 + dot(pick, lower.astype(BF16))
    degree = jnp.sum(jnp.where((node & 31) == lane, spread, 0.0), axis=1, keepdims=True)
    inverse = 1.0 / jnp.maximum(degree, 1.0)
    x = (inverse * cot[...].astype(F32)).astype(BF16)
    x_out[...] = x
    for g in range(ngroup):
        rows_out[g] = dot(marked[g], x, DOWN).astype(BF16)


def build(edges, tile_out, acc):
    nodes = acc.shape[0]
    acc[...] = jnp.zeros_like(acc)
    live = jnp.sum((edges[0] >= 0).astype(I32))

    def step(i, carry):
        packed = edges[0, :, pl.ds(pl.multiple_of(i * CHUNK, CHUNK), CHUNK)]
        acc[...] += dot(small_hot(nodes, packed >> 10), small_hot(nodes, packed & 1023), ALONG)
        return carry

    lax.fori_loop(0, (live + CHUNK - 1) // CHUNK, step, 0)
    tile_out[0] = acc[...].astype(BF16)


def first_sum(tile0, tile1, x0, x1, ids, rows, out):
    i = pl.program_id(0)
    block = out.shape[0]
    total = dot(tile0[0], x0[...]) + dot(tile1[0], x1[...])
    spots = lax.broadcasted_iota(I32, (block, ids.shape[1]), 0) + i * block
    sel = jnp.where(spots == ids[...], 1.0, 0.0).astype(BF16)
    out[...] = total + dot(sel, rows[...])


def middle_sum(before, t0, t1, t2, t3, x0, x1, x2, x3, out):
    total = before[...] + dot(t0[0], x0[...]) + dot(t1[0], x1[...])
    out[...] = total + dot(t2[0], x2[...]) + dot(t3[0], x3[...])


def last_sum(before, t0, t1, x0, x1, feats, out, send, keep, grad):
    nodes = before.shape[0]
    for i in range(nodes // BLOCK):
        rows = slice(i * BLOCK, (i + 1) * BLOCK)
        total = before[rows, :] + dot(t0[0, rows, :], x0[...]) + dot(t1[0, rows, :], x1[...])
        out[rows, :] = total
        top = total.astype(BF16)
        rest = (total - top.astype(F32)).astype(BF16)
        part = dot(feats[rows, :], top, DOWN) + dot(feats[rows, :], rest, DOWN)
        if i == 0:
            grad[...] = part
        else:
            grad[...] += part
    half = send.shape[0]
    core = lax.axis_index("core")
    keep[...] = grad[pl.ds(pl.multiple_of(core * half, half), half), :]
    send[...] = grad[pl.ds(pl.multiple_of((1 - core) * half, half), half), :]


def place(factor, *refs):
    out_self, out_neigh = refs[-2], refs[-1]
    ngroup = (len(refs) - 2) // 2
    ny, _, size, _ = refs[0].shape
    group, core, ypos = (lax.axis_index(a) for a in ("group", "core", "y"))
    for n in range(2 * ngroup):
        k = core if n < ngroup else 1 - core
        g = lax.rem(group - n % ngroup + ngroup, ngroup)
        for t in range(ny):
            y = lax.rem(ypos - t + ny, ny)
            at = pl.multiple_of(((k * ngroup + g) * ny + y) * size, size)
            out_self[pl.ds(at, size), :] = refs[n][t, 0] * factor
            out_neigh[pl.ds(at, size), :] = refs[n][t, 1] * factor


def finish(summed, cot, w_self, w_neigh, out):
    total = summed[...]
    top = total.astype(BF16)
    rest = (total - top.astype(F32)).astype(BF16)
    out[...] = (
        dot(cot[...], w_self[...], ALONG)
        + dot(top, w_neigh[...], ALONG)
        + dot(rest, w_neigh[...], ALONG)
    )


BLOCK = 256
MIB = 1024 * 1024


def params(mib):
    return pltpu.CompilerParams(vmem_limit_bytes=mib * MIB)


def whole(shape):
    return pl.BlockSpec(shape, lambda i: (0,) * len(shape))


def tile_spec(slot, nodes):
    return pl.BlockSpec((1, BLOCK, nodes), lambda i: (slot, i, 0))


def row_spec(width):
    return pl.BlockSpec((BLOCK, width), lambda i: (i, 0))


def estimate(macs, moved):
    return pl.CostEstimate(flops=2 * macs, bytes_accessed=moved, transcendentals=0)


def run_whole(kernel, given, made, macs, name):
    return pl.pallas_call(
        kernel,
        grid=(1,),
        out_shape=[jax.ShapeDtypeStruct(*m) for m in made],
        in_specs=[whole(v.shape) for v in given],
        out_specs=[whole(m[0]) for m in made],
        compiler_params=params(63),
        cost_estimate=estimate(macs, sum(2 * v.size for v in given)),
        name=name,
    )(*given)


def run_build(edges, nodes):
    slots, _, ept = edges.shape
    return pl.pallas_call(
        build,
        grid=(slots,),
        in_specs=[pl.BlockSpec((1, 1, ept), lambda s: (s, 0, 0))],
        out_specs=pl.BlockSpec((1, nodes, nodes), lambda s: (s, 0, 0)),
        scratch_shapes=[pltpu.VMEM((nodes, nodes), F32)],
        out_shape=jax.ShapeDtypeStruct((slots, nodes, nodes), BF16),
        compiler_params=params(60),
        cost_estimate=estimate(slots * nodes * nodes * ept // 16, 2 * slots * nodes * nodes),
        name="build",
    )(edges)


def run_first(tiles, x0, x1, ids, rows):
    nodes, width = x0.shape
    return pl.pallas_call(
        first_sum,
        grid=(nodes // BLOCK,),
        in_specs=[
            tile_spec(0, nodes),
            tile_spec(1, nodes),
            whole(x0.shape),
            whole(x1.shape),
            whole(ids.shape),
            whole(rows.shape),
        ],
        out_specs=row_spec(width),
        out_shape=jax.ShapeDtypeStruct((nodes, width), F32),
        compiler_params=params(36),
        cost_estimate=estimate(3 * nodes * nodes * width, 12 * nodes * width),
        name="first_sum",
    )(tiles, tiles, x0, x1, ids, rows)


def run_middle(before, own, other, xs):
    nodes, width = before.shape
    return pl.pallas_call(
        middle_sum,
        grid=(nodes // BLOCK,),
        in_specs=[row_spec(width)]
        + [tile_spec(s, nodes) for s in (0, 1, 0, 1)]
        + [whole(x.shape) for x in xs],
        out_specs=row_spec(width),
        out_shape=jax.ShapeDtypeStruct((nodes, width), F32),
        compiler_params=params(36),
        cost_estimate=estimate(4 * nodes * nodes * width, 16 * nodes * width),
        name="middle_sum",
    )(before, own, own, other, other, *xs)


def run_last(before, own, other, xs, features):
    nodes, width = before.shape
    vm = pl.BlockSpec(memory_space=pltpu.VMEM)
    return pl.pallas_call(
        last_sum,
        in_specs=[vm] * 6,
        out_specs=[vm] * 3,
        out_shape=(
            jax.ShapeDtypeStruct((nodes, width), F32),
            jax.ShapeDtypeStruct((width // 2, width), F32),
            jax.ShapeDtypeStruct((width // 2, width), F32),
        ),
        scratch_shapes=[pltpu.VMEM((width, width), F32)],
        compiler_params=params(24),
        cost_estimate=estimate(3 * nodes * nodes * width, 16 * nodes * width),
        name="last_sum",
    )(before, own, other, *xs, features)


def run_place(pieces, factor, width):
    return pl.pallas_call(
        lambda *refs: place(factor, *refs),
        grid=(1,),
        in_specs=[whole(v.shape) for v in pieces],
        out_specs=[whole((width, width))] * 2,
        out_shape=[jax.ShapeDtypeStruct((width, width), F32)] * 2,
        compiler_params=params(24),
        cost_estimate=estimate(width * width, 16 * width * width),
        name="place",
    )(*pieces)


def run_finish(summed, cotangent, w_self, w_neigh):
    nodes, width = summed.shape
    return pl.pallas_call(
        finish,
        grid=(nodes // BLOCK,),
        in_specs=[row_spec(width), row_spec(width), whole(w_self.shape), whole(w_neigh.shape)],
        out_specs=row_spec(width),
        out_shape=jax.ShapeDtypeStruct((nodes, width), F32),
        compiler_params=params(24),
        cost_estimate=estimate(3 * nodes * width * width, 10 * nodes * width),
        name="finish",
    )(summed, cotangent, w_self, w_neigh)


BLK = ("z", "y", "core")


def moved(value, perm):
    return lax.ppermute(value, BLK, perm)


def turned(value, axis, by):
    length = lax.axis_size(axis)
    return lax.ppermute(value, axis, [(i, (i + by) % length) for i in range(length)])


def fence(values):
    return lax.optimization_barrier(values)


def on_device(
    features,
    cotangent,
    w_self,
    w_neigh,
    tile_src,
    tile_dst,
    tile_count,
    send_ids,
    recv_dst,
    recv_count,
):
    nodes, width = features.shape
    ngroup, cap = send_ids.shape[1], send_ids.shape[2]
    ept = tile_src.shape[2]
    nz, ny = lax.axis_size("z"), lax.axis_size("y")
    nblk = nz * ny * 2
    core, ypos = lax.axis_index("core"), lax.axis_index("y")
    ring = range(nblk)
    swap = [(0, 1), (1, 0)]

    def swapped(v):
        return lax.ppermute(v, "core", swap)

    own, first, pair1, pair2, pair3 = run_whole(
        pack,
        (tile_count, tile_src, tile_dst),
        [((1, ept), I32)] * 2 + [((2, ept), I32)] * 3,
        8 * ept,
        "pack",
    )
    first = moved(first, [(i, (i - 1 if i % 2 else i - 7) % nblk) for i in ring])
    pairs = [
        moved(p, [(i, (i - 2 * j) % nblk) for i in ring])
        for j, p in ((1, pair1), (2, pair2), (3, pair3))
    ]
    x, rows = run_whole(
        prepare,
        (tile_count, recv_count, tile_dst, recv_dst, cotangent),
        [((nodes, width), BF16), ((ngroup, cap, width), BF16)],
        ngroup * cap * nodes * width,
        "prepare",
    )
    x, own, first, pairs = fence((x, own, first, pairs))
    far = turned(x, "z", -1)
    other = swapped(jnp.concatenate([p[1:2] for p in pairs], axis=0))
    self_part = dot(features, cotangent, DOWN)
    half = width // 2
    self_part = jnp.where(core == 0, self_part[:half], self_part[half:]) + swapped(
        jnp.where(core == 0, self_part[half:], self_part[:half])
    )
    near = run_build(jnp.stack([own, first]), nodes)
    rows = fence((rows, near))[0]
    returned = lax.all_to_all(rows, "group", split_axis=0, concat_axis=0, tiled=True)
    mine = run_build(jnp.stack([pairs[0][0:1], pairs[2][0:1]]), nodes)
    mid_own = run_build(pairs[1][None, 0:1], nodes)
    x, far = fence((x, far, near, mine, mid_own, self_part, other))[:2]

    one = turned(jnp.where(ypos == 0, far, x), "y", -1)
    three = turned(jnp.where(ypos == ny - 1, x, far), "y", 1)
    side = swapped(jnp.where(core == 1, x, far))
    theirs = run_build(jnp.stack([other[0:1], other[2:3]]), nodes)
    mid_other = run_build(other[None, 1:2], nodes)
    summed = run_first(
        near, x, side, send_ids.reshape(1, ngroup * cap), returned.reshape(ngroup * cap, width)
    )
    one, three = fence((one, three, theirs, mid_own, mid_other, summed))[:2]

    two = moved(
        jnp.where(core == 0, one, three),
        [(i, (i - 2 if i % 2 == 0 else i + 2) % nblk) for i in ring],
    )
    one_b = swapped(one)
    three_b = swapped(three)
    summed = run_middle(summed, mine, theirs, (one, three, one_b, three_b))
    two = fence((two, summed))[0]

    two_b = swapped(two)
    summed, send, keep = run_last(summed, mid_own, mid_other, (two, two_b), features)

    part = keep + swapped(send)
    size = half // ngroup // ny
    part = jnp.stack([self_part, part]).reshape(2, ngroup * ny, size, width).transpose(1, 0, 2, 3)
    part = lax.all_to_all(part, ("group", "y"), split_axis=0, concat_axis=0, tiled=True).sum(0)

    def zflip(v, k):
        return lax.ppermute(v, "z", [(i, i ^ k) for i in range(nz)])

    part = (part + zflip(part, 1)) + (zflip(part, 2) + zflip(part, 3))
    part = part + zflip(part, 4)
    part = jnp.stack([part] + [turned(part, "y", t) for t in range(1, ny)])
    held = [part] + [turned(part, "group", s) for s in range(1, ngroup)]
    held = held + [swapped(v) for v in held]
    total = run_finish(summed, cotangent, w_self, w_neigh)
    factor = 1.0 / math.sqrt(nodes * ngroup * nblk)
    grad_self, grad_neigh = run_place(held, factor, width)
    return (total, grad_self, grad_neigh)


def solution(mesh):
    blk = mesh.shape["blk"]
    fine = Mesh(
        mesh.devices.reshape(mesh.shape["group"], blk // 8, 4, 2), ("group",) + BLK
    )
    both = ("group",) + BLK
    placed = (
        P(both, None),
        P(both, None),
        P(),
        P(),
        P(both, None, None),
        P(both, None, None),
        P(both, None),
        P(both, None, None),
        P(both, None, None),
        P(both, None),
    )
    return jax.shard_map(
        on_device,
        mesh=fine,
        in_specs=placed,
        out_specs=(P(both, None), P(), P()),
        check_vma=False,
    )
```

```python
import functools
import math

import jax
import jax.numpy as jnp
from jax import lax
from jax.experimental import pallas as pl
from jax.experimental.pallas import tpu as pltpu
from jax.sharding import Mesh
from jax.sharding import PartitionSpec as P

F32 = jnp.float32
BF16 = jnp.bfloat16
I32 = jnp.int32
CHUNK = 1024
ALONG = (((1,), (1,)), ((), ()))
DOWN = (((0,), (0,)), ((), ()))


def dot(a, b, dims=(((1,), (0,)), ((), ()))):
    return lax.dot_general(a, b, dims, preferred_element_type=F32)


def hot(rows, ids):
    spots = lax.broadcasted_iota(I32, (rows, ids.shape[1]), 0)
    return jnp.where(spots == ids, 1.0, 0.0).astype(BF16)


def small_hot(rows, ids):
    spots = lax.broadcasted_iota(jnp.int16, (rows, ids.shape[1]), 0)
    ones = jnp.where(spots == ids.astype(jnp.int16), jnp.ones((), BF16), jnp.zeros((), BF16))
    return ones.astype(jnp.float8_e4m3fn)


def prepare(
    tcount, rcount, tsrc, tdst, rdst, cot, x_out, rows_out, own, first, pair1, pair2, pair3
):
    nodes = cot.shape[0]
    odd = lax.axis_index("core") == 1
    offs, ept = tdst.shape[1], tdst.shape[2]
    ngroup, cap = rdst.shape[1], rdst.shape[2]
    slot = lax.broadcasted_iota(I32, (1, ept), 1)
    counts = jnp.zeros((32, 32), F32)
    lists = []
    for s in range(offs):
        live = slot < tcount[0:1, s : s + 1]
        ids = jnp.where(live, tdst[0, s : s + 1, :], 1023)
        counts = counts + dot(hot(32, ids >> 5), hot(32, ids & 31), ALONG)
        lists.append(jnp.where(live, tsrc[0, s : s + 1, :] * 1024 + ids, -1))
    own[...] = lists[0]
    first[...] = jnp.where(odd, lists[1], lists[7])
    for j, pair in ((1, pair1), (2, pair2), (3, pair3)):
        pair[0:1, :] = lists[2 * j]
        pair[1:2, :] = jnp.where(odd, lists[2 * j + 1], lists[2 * j - 1])
    slot = lax.broadcasted_iota(I32, (1, cap), 1)
    marked = []
    for g in range(ngroup):
        ids = jnp.where(slot < rcount[0:1, g : g + 1], rdst[0, g : g + 1, :], 1023)
        counts = counts + dot(hot(32, ids >> 5), hot(32, ids & 31), ALONG)
        marked.append(hot(nodes, ids))
    upper = jnp.floor(counts * (1.0 / 128.0))
    lower = counts - upper * 128.0
    node = lax.broadcasted_iota(I32, (nodes, 32), 0)
    lane = lax.broadcasted_iota(I32, (nodes, 32), 1)
    pick = jnp.where((node >> 5) == lane, 1.0, 0.0).astype(BF16)
    spread = dot(pick, upper.astype(BF16)) * 128.0 + dot(pick, lower.astype(BF16))
    degree = jnp.sum(jnp.where((node & 31) == lane, spread, 0.0), axis=1, keepdims=True)
    inverse = 1.0 / jnp.maximum(degree, 1.0)
    x = (inverse * cot[...].astype(F32)).astype(BF16)
    x_out[...] = x
    for g in range(ngroup):
        rows_out[g] = dot(marked[g], x, DOWN).astype(BF16)


def build(rows, *refs):
    lists, (tile_out, acc, edges) = refs[:-3], refs[-3:]
    s = pl.program_id(0)
    nodes = acc.shape[0]

    @pl.when(s == 0)
    def _():
        for k, row in enumerate(rows):
            edges[k] = lists[k][row : row + 1, :]

    acc[...] = jnp.zeros_like(acc)
    live = jnp.sum((edges[s] >= 0).astype(I32))

    def step(i, carry):
        packed = edges[s, :, pl.ds(pl.multiple_of(i * CHUNK, CHUNK), CHUNK)]
        acc[...] += dot(small_hot(nodes, packed >> 10), small_hot(nodes, packed & 1023), ALONG)
        return carry

    lax.fori_loop(0, (live + CHUNK - 1) // CHUNK, step, 0)
    tile_out[0] = acc[...].astype(BF16)


def most_sum(t0, t1, t2, t3, t4, t5, x0, x1, x2, x3, x4, x5, ids, rows, out):
    i = pl.program_id(0)
    block = out.shape[0]
    spots = lax.broadcasted_iota(I32, (block, ids.shape[1]), 0) + i * block
    total = dot(jnp.where(spots == ids[...], 1.0, 0.0).astype(BF16), rows[...])
    for tile, x in ((t0, x0), (t1, x1), (t2, x2), (t3, x3), (t4, x4), (t5, x5)):
        total = total + dot(tile[0], x[...])
    out[...] = total


def last_sum(before, tiles, x0, x1, feats, cot, out, send, keep, grad_self, grad_neigh):
    nodes = before.shape[0]
    grad_self[...] = dot(feats[...], cot[...], DOWN)
    for i in range(nodes // BLOCK):
        rows = slice(i * BLOCK, (i + 1) * BLOCK)
        total = before[rows, :] + dot(tiles[0, rows, :], x0[...])
        total = total + dot(tiles[1, rows, :], x1[...])
        out[rows, :] = total
        top = total.astype(BF16)
        rest = (total - top.astype(F32)).astype(BF16)
        part = dot(feats[rows, :], top, DOWN) + dot(feats[rows, :], rest, DOWN)
        if i == 0:
            grad_neigh[...] = part
        else:
            grad_neigh[...] += part
    pieces, _, size, _ = send.shape
    core = lax.axis_index("core")
    for n in range(pieces):
        here = pl.ds(pl.multiple_of((core * pieces + n) * size, size), size)
        there = pl.ds(pl.multiple_of(((1 - core) * pieces + n) * size, size), size)
        for m, grad in enumerate((grad_self, grad_neigh)):
            keep[n, m] = grad[here, :]
            send[n, m] = grad[there, :]


def place(factor, *refs):
    out_self, out_neigh = refs[-2], refs[-1]
    ngroup = (len(refs) - 2) // 2
    ny, _, size, _ = refs[0].shape
    group, core, ypos = (lax.axis_index(a) for a in ("group", "core", "y"))
    for n in range(2 * ngroup):
        k = core if n < ngroup else 1 - core
        g = lax.rem(group - n % ngroup + ngroup, ngroup)
        for t in range(ny):
            y = lax.rem(ypos - t + ny, ny)
            at = pl.multiple_of(((k * ngroup + g) * ny + y) * size, size)
            out_self[pl.ds(at, size), :] = refs[n][t, 0] * factor
            out_neigh[pl.ds(at, size), :] = refs[n][t, 1] * factor


def finish(summed, cot, w_self, w_neigh, out):
    total = summed[...]
    top = total.astype(BF16)
    rest = (total - top.astype(F32)).astype(BF16)
    out[...] = (
        dot(cot[...], w_self[...], ALONG)
        + dot(top, w_neigh[...], ALONG)
        + dot(rest, w_neigh[...], ALONG)
    )


BLOCK = 256
MIB = 1024 * 1024


def params(mib):
    return pltpu.CompilerParams(vmem_limit_bytes=mib * MIB)


def whole(shape):
    return pl.BlockSpec(shape, lambda i: (0,) * len(shape))


def tile_spec(slot, nodes):
    return pl.BlockSpec((1, BLOCK, nodes), lambda i: (slot, i, 0))


def row_spec(width):
    return pl.BlockSpec((BLOCK, width), lambda i: (i, 0))


def estimate(macs, moved):
    return pl.CostEstimate(flops=2 * macs, bytes_accessed=moved, transcendentals=0)


def run_whole(kernel, given, made, macs, name):
    return pl.pallas_call(
        kernel,
        grid=(1,),
        out_shape=[jax.ShapeDtypeStruct(*m) for m in made],
        in_specs=[whole(v.shape) for v in given],
        out_specs=[whole(m[0]) for m in made],
        compiler_params=params(63),
        cost_estimate=estimate(macs, sum(2 * v.size for v in given)),
        name=name,
    )(*given)


def run_build(chosen, nodes):
    slots, ept = len(chosen), chosen[0][0].shape[1]
    rows = tuple(row for _, row in chosen)
    lists = [v for v, _ in chosen]
    return pl.pallas_call(
        functools.partial(build, rows),
        grid=(slots,),
        in_specs=[whole(v.shape) for v in lists],
        out_specs=pl.BlockSpec((1, nodes, nodes), lambda s: (s, 0, 0)),
        scratch_shapes=[pltpu.VMEM((nodes, nodes), F32), pltpu.VMEM((slots, 1, ept), I32)],
        out_shape=jax.ShapeDtypeStruct((slots, nodes, nodes), BF16),
        compiler_params=params(60),
        cost_estimate=estimate(nodes * ept, nodes * ept),
        name="build",
    )(*lists)


def run_most(near, quad, xs, ids, rows):
    nodes, width = xs[0].shape
    return pl.pallas_call(
        most_sum,
        grid=(nodes // BLOCK,),
        in_specs=[tile_spec(s, nodes) for s in (0, 1, 0, 1, 2, 3)]
        + [whole(v.shape) for v in (*xs, ids, rows)],
        out_specs=row_spec(width),
        out_shape=jax.ShapeDtypeStruct((nodes, width), F32),
        compiler_params=params(36),
        cost_estimate=estimate(7 * nodes * nodes * width, 16 * nodes * width),
        name="most_sum",
    )(near, near, quad, quad, quad, quad, *xs, ids, rows)


def run_last(before, tiles, xs, features, cotangent, pieces):
    nodes, width = before.shape
    vm = pl.BlockSpec(memory_space=pltpu.VMEM)
    half = jax.ShapeDtypeStruct((pieces, 2, width // (2 * pieces), width), F32)
    return pl.pallas_call(
        last_sum,
        in_specs=[vm] * 6,
        out_specs=[vm] * 3,
        out_shape=(jax.ShapeDtypeStruct((nodes, width), F32), half, half),
        scratch_shapes=[pltpu.VMEM((width, width), F32)] * 2,
        compiler_params=params(24),
        cost_estimate=estimate(3 * nodes * nodes * width, 16 * nodes * width),
        name="last_sum",
    )(before, tiles, *xs, features, cotangent)


def run_place(pieces, factor, width):
    return pl.pallas_call(
        lambda *refs: place(factor, *refs),
        grid=(1,),
        in_specs=[whole(v.shape) for v in pieces],
        out_specs=[whole((width, width))] * 2,
        out_shape=[jax.ShapeDtypeStruct((width, width), F32)] * 2,
        compiler_params=params(24),
        cost_estimate=estimate(width * width, 16 * width * width),
        name="place",
    )(*pieces)


def run_finish(summed, cotangent, w_self, w_neigh):
    nodes, width = summed.shape
    return pl.pallas_call(
        finish,
        grid=(nodes // BLOCK,),
        in_specs=[row_spec(width), row_spec(width), whole(w_self.shape), whole(w_neigh.shape)],
        out_specs=row_spec(width),
        out_shape=jax.ShapeDtypeStruct((nodes, width), F32),
        compiler_params=params(24),
        cost_estimate=estimate(3 * nodes * width * width, 10 * nodes * width),
        name="finish",
    )(summed, cotangent, w_self, w_neigh)


BLK = ("z", "y", "core")


def moved(value, perm):
    return lax.ppermute(value, BLK, perm)


def turned(value, axis, by):
    length = lax.axis_size(axis)
    return lax.ppermute(value, axis, [(i, (i + by) % length) for i in range(length)])


def fence(values):
    return lax.optimization_barrier(values)


def on_device(
    features,
    cotangent,
    w_self,
    w_neigh,
    tile_src,
    tile_dst,
    tile_count,
    send_ids,
    recv_dst,
    recv_count,
):
    nodes, width = features.shape
    ngroup, cap = send_ids.shape[1], send_ids.shape[2]
    ept = tile_src.shape[2]
    nz, ny = lax.axis_size("z"), lax.axis_size("y")
    nblk = nz * ny * 2
    core, ypos = lax.axis_index("core"), lax.axis_index("y")
    ring = range(nblk)
    swap = [(0, 1), (1, 0)]

    def swapped(v):
        return lax.ppermute(v, "core", swap)

    x, rows, own, first, pair1, pair2, pair3 = run_whole(
        prepare,
        (tile_count, recv_count, tile_src, tile_dst, recv_dst, cotangent),
        [((nodes, width), BF16), ((ngroup, cap, width), BF16)]
        + [((1, ept), I32)] * 2
        + [((2, ept), I32)] * 3,
        ngroup * cap * nodes * width,
        "prepare",
    )
    far = turned(x, "z", -1)
    first = moved(first, [(i, (i - 1 if i % 2 else i - 7) % nblk) for i in ring])
    pairs = [
        moved(p, [(i, (i - 2 * j) % nblk) for i in ring])
        for j, p in ((1, pair1), (2, pair2), (3, pair3))
    ]
    rows = fence((rows, first))[0]
    returned = lax.all_to_all(rows, "group", split_axis=0, concat_axis=0, tiled=True)
    x, far = fence((x, far, first, pairs))[:2]

    one = turned(jnp.where(ypos == 0, far, x), "y", -1)
    three = turned(jnp.where(ypos == ny - 1, x, far), "y", 1)
    side = swapped(jnp.where(core == 1, x, far))
    other = swapped(jnp.concatenate([p[1:2] for p in pairs], axis=0))
    near = run_build(((own, 0), (first, 0)), nodes)
    quad = run_build(((pairs[0], 0), (pairs[2], 0), (other, 0), (other, 2)), nodes)
    mid = run_build(((pairs[1], 0), (other, 1)), nodes)
    one, three = fence((one, three, near, quad, mid, side))[:2]
    relay = jnp.where(core == 0, one, three)

    two = moved(
        relay,
        [(i, (i - 2 if i % 2 == 0 else i + 2) % nblk) for i in ring],
    )
    one_b = swapped(one)
    three_b = swapped(three)
    summed = run_most(
        near,
        quad,
        (x, side, one, three, one_b, three_b),
        send_ids.reshape(1, ngroup * cap),
        returned.reshape(ngroup * cap, width),
    )
    two = fence((two, summed))[0]

    two_b = swapped(two)
    summed, send, keep = run_last(
        summed, mid, (two, two_b), features, cotangent, ngroup * ny
    )

    part = keep + swapped(send)
    part = lax.all_to_all(part, ("group", "y"), split_axis=0, concat_axis=0, tiled=True).sum(0)

    def zflip(v, k):
        return lax.ppermute(v, "z", [(i, i ^ k) for i in range(nz)])

    part = (part + zflip(part, 1)) + (zflip(part, 2) + zflip(part, 3))
    part, total = fence((part, run_finish(summed, cotangent, w_self, w_neigh)))
    part = part + zflip(part, 4)
    part = jnp.stack([part] + [turned(part, "y", t) for t in range(1, ny)])
    held = [part] + [turned(part, "group", s) for s in range(1, ngroup)]
    held = held + [swapped(v) for v in held]
    factor = 1.0 / math.sqrt(nodes * ngroup * nblk)
    grad_self, grad_neigh = run_place(held, factor, width)
    return (total, grad_self, grad_neigh)


def solution(mesh):
    blk = mesh.shape["blk"]
    fine = Mesh(
        mesh.devices.reshape(mesh.shape["group"], blk // 8, 4, 2), ("group",) + BLK
    )
    both = ("group",) + BLK
    placed = (
        P(both, None),
        P(both, None),
        P(),
        P(),
        P(both, None, None),
        P(both, None, None),
        P(both, None),
        P(both, None, None),
        P(both, None, None),
        P(both, None),
    )
    return jax.shard_map(
        on_device,
        mesh=fine,
        in_specs=placed,
        out_specs=(P(both, None), P(), P()),
        check_vma=False,
    )
```

```python
import functools
import math

import jax
import jax.numpy as jnp
from jax import lax
from jax.experimental import pallas as pl
from jax.experimental.pallas import tpu as pltpu
from jax.sharding import Mesh
from jax.sharding import PartitionSpec as P

F32 = jnp.float32
BF16 = jnp.bfloat16
I32 = jnp.int32
CHUNK = 512
ALONG = (((1,), (1,)), ((), ()))
DOWN = (((0,), (0,)), ((), ()))


def dot(a, b, dims=(((1,), (0,)), ((), ()))):
    return lax.dot_general(a, b, dims, preferred_element_type=F32)


def hot(rows, ids):
    spots = lax.broadcasted_iota(I32, (rows, ids.shape[1]), 0)
    return jnp.where(spots == ids, 1.0, 0.0).astype(BF16)


def small_hot(rows, ids):
    spots = lax.broadcasted_iota(jnp.int16, (rows, ids.shape[1]), 0)
    ones = jnp.where(spots == ids.astype(jnp.int16), jnp.ones((), BF16), jnp.zeros((), BF16))
    return ones.astype(jnp.float8_e4m3fn)


def prepare(
    tcount, rcount, tsrc, tdst, rdst, cot, x_out, rows_out, own, first, pair1, pair2, pair3
):
    nodes = cot.shape[0]
    odd = lax.axis_index("core") == 1
    offs, ept = tdst.shape[1], tdst.shape[2]
    ngroup, cap = rdst.shape[1], rdst.shape[2]
    slot = lax.broadcasted_iota(I32, (1, ept), 1)
    counts = jnp.zeros((32, 32), F32)
    lists = []
    for s in range(offs):
        live = slot < tcount[0:1, s : s + 1]
        ids = jnp.where(live, tdst[0, s : s + 1, :], 1023)
        counts = counts + dot(hot(32, ids >> 5), hot(32, ids & 31), ALONG)
        lists.append(jnp.where(live, tsrc[0, s : s + 1, :] * 1024 + ids, -1))
    own[...] = lists[0]
    first[...] = jnp.where(odd, lists[1], lists[7])
    for j, pair in ((1, pair1), (2, pair2), (3, pair3)):
        pair[0:1, :] = lists[2 * j]
        pair[1:2, :] = jnp.where(odd, lists[2 * j + 1], lists[2 * j - 1])
    slot = lax.broadcasted_iota(I32, (1, cap), 1)
    marked = []
    for g in range(ngroup):
        ids = jnp.where(slot < rcount[0:1, g : g + 1], rdst[0, g : g + 1, :], 1023)
        counts = counts + dot(hot(32, ids >> 5), hot(32, ids & 31), ALONG)
        marked.append(hot(nodes, ids))
    upper = jnp.floor(counts * (1.0 / 128.0))
    lower = counts - upper * 128.0
    node = lax.broadcasted_iota(I32, (nodes, 32), 0)
    lane = lax.broadcasted_iota(I32, (nodes, 32), 1)
    pick = jnp.where((node >> 5) == lane, 1.0, 0.0).astype(BF16)
    spread = dot(pick, upper.astype(BF16)) * 128.0 + dot(pick, lower.astype(BF16))
    degree = jnp.sum(jnp.where((node & 31) == lane, spread, 0.0), axis=1, keepdims=True)
    inverse = 1.0 / jnp.maximum(degree, 1.0)
    x = (inverse * cot[...].astype(F32)).astype(BF16)
    x_out[...] = x
    for g in range(ngroup):
        rows_out[g] = dot(marked[g], x, DOWN).astype(BF16)


def build(rows, *refs):
    lists, (tile_out, edges) = refs[:-2], refs[-2:]
    s = pl.program_id(0)
    nodes, ept = tile_out.shape[1], edges.shape[2]

    @pl.when(s == 0)
    def _():
        for k, row in enumerate(rows):
            edges[k] = lists[k][row : row + 1, :]

    live = jnp.sum((edges[s] >= 0).astype(I32))
    for low in range(0, ept, CHUNK):
        @pl.when((live <= low + CHUNK) & ((live > low) | (low == 0)))
        def _():
            packed = edges[s, :, : low + CHUNK]
            tile = dot(small_hot(nodes, packed >> 10), small_hot(nodes, packed & 1023), ALONG)
            tile_out[0] = tile.astype(BF16)


def most_sum(t0, t1, t2, t3, t4, t5, x0, x1, x2, x3, x4, x5, ids, rows, out):
    i = pl.program_id(0)
    block = out.shape[0]
    spots = lax.broadcasted_iota(I32, (block, ids.shape[1]), 0) + i * block
    total = dot(jnp.where(spots == ids[...], 1.0, 0.0).astype(BF16), rows[...])
    for tile, x in ((t0, x0), (t1, x1), (t2, x2), (t3, x3), (t4, x4), (t5, x5)):
        total = total + dot(tile[0], x[...])
    out[...] = total


def last_sum(before, tiles, x0, x1, feats, cot, out, send, keep, grad_self, grad_neigh):
    nodes = before.shape[0]
    grad_self[...] = dot(feats[...], cot[...], DOWN)
    for i in range(nodes // BLOCK):
        rows = slice(i * BLOCK, (i + 1) * BLOCK)
        total = before[rows, :] + dot(tiles[0, rows, :], x0[...])
        total = total + dot(tiles[1, rows, :], x1[...])
        out[rows, :] = total
        top = total.astype(BF16)
        rest = (total - top.astype(F32)).astype(BF16)
        part = dot(feats[rows, :], top, DOWN) + dot(feats[rows, :], rest, DOWN)
        if i == 0:
            grad_neigh[...] = part
        else:
            grad_neigh[...] += part
    pieces, _, size, _ = send.shape
    core = lax.axis_index("core")
    for n in range(pieces):
        here = pl.ds(pl.multiple_of((core * pieces + n) * size, size), size)
        there = pl.ds(pl.multiple_of(((1 - core) * pieces + n) * size, size), size)
        for m, grad in enumerate((grad_self, grad_neigh)):
            keep[n, m] = grad[here, :]
            send[n, m] = grad[there, :]


def place(factor, *refs):
    out_self, out_neigh = refs[-2], refs[-1]
    ngroup = (len(refs) - 2) // 2
    ny, _, size, _ = refs[0].shape
    group, core, ypos = (lax.axis_index(a) for a in ("group", "core", "y"))
    for n in range(2 * ngroup):
        k = core if n < ngroup else 1 - core
        g = lax.rem(group - n % ngroup + ngroup, ngroup)
        for t in range(ny):
            y = lax.rem(ypos - t + ny, ny)
            at = pl.multiple_of(((k * ngroup + g) * ny + y) * size, size)
            out_self[pl.ds(at, size), :] = refs[n][t, 0] * factor
            out_neigh[pl.ds(at, size), :] = refs[n][t, 1] * factor


def finish(summed, cot, w_self, w_neigh, out):
    total = summed[...]
    top = total.astype(BF16)
    rest = (total - top.astype(F32)).astype(BF16)
    out[...] = (
        dot(cot[...], w_self[...], ALONG)
        + dot(top, w_neigh[...], ALONG)
        + dot(rest, w_neigh[...], ALONG)
    )


BLOCK = 256
MIB = 1024 * 1024


def params(mib):
    return pltpu.CompilerParams(vmem_limit_bytes=mib * MIB)


def whole(shape):
    return pl.BlockSpec(shape, lambda i: (0,) * len(shape))


def tile_spec(slot, nodes):
    return pl.BlockSpec((1, BLOCK, nodes), lambda i: (slot, i, 0))


def row_spec(width):
    return pl.BlockSpec((BLOCK, width), lambda i: (i, 0))


def estimate(macs, moved):
    return pl.CostEstimate(flops=2 * macs, bytes_accessed=moved, transcendentals=0)


def run_whole(kernel, given, made, macs, name):
    return pl.pallas_call(
        kernel,
        grid=(1,),
        out_shape=[jax.ShapeDtypeStruct(*m) for m in made],
        in_specs=[whole(v.shape) for v in given],
        out_specs=[whole(m[0]) for m in made],
        compiler_params=params(63),
        cost_estimate=estimate(macs, sum(2 * v.size for v in given)),
        name=name,
    )(*given)


def run_build(chosen, nodes):
    slots, ept = len(chosen), chosen[0][0].shape[1]
    rows = tuple(row for _, row in chosen)
    lists = [v for v, _ in chosen]
    return pl.pallas_call(
        functools.partial(build, rows),
        grid=(slots,),
        in_specs=[whole(v.shape) for v in lists],
        out_specs=pl.BlockSpec((1, nodes, nodes), lambda s: (s, 0, 0)),
        scratch_shapes=[pltpu.VMEM((slots, 1, ept), I32)],
        out_shape=jax.ShapeDtypeStruct((slots, nodes, nodes), BF16),
        compiler_params=params(60),
        cost_estimate=estimate(nodes * ept, nodes * ept),
        name="build",
    )(*lists)


def run_most(near, quad, xs, ids, rows):
    nodes, width = xs[0].shape
    return pl.pallas_call(
        most_sum,
        grid=(nodes // BLOCK,),
        in_specs=[tile_spec(s, nodes) for s in (0, 1, 0, 1, 2, 3)]
        + [whole(v.shape) for v in (*xs, ids, rows)],
        out_specs=row_spec(width),
        out_shape=jax.ShapeDtypeStruct((nodes, width), F32),
        compiler_params=params(56),
        cost_estimate=estimate(7 * nodes * nodes * width, 16 * nodes * width),
        name="most_sum",
    )(near, near, quad, quad, quad, quad, *xs, ids, rows)


def run_last(before, tiles, xs, features, cotangent, pieces):
    nodes, width = before.shape
    vm = pl.BlockSpec(memory_space=pltpu.VMEM)
    half = jax.ShapeDtypeStruct((pieces, 2, width // (2 * pieces), width), F32)
    return pl.pallas_call(
        last_sum,
        in_specs=[vm] * 6,
        out_specs=[vm] * 3,
        out_shape=(jax.ShapeDtypeStruct((nodes, width), F32), half, half),
        scratch_shapes=[pltpu.VMEM((width, width), F32)] * 2,
        compiler_params=params(24),
        cost_estimate=estimate(3 * nodes * nodes * width, 16 * nodes * width),
        name="last_sum",
    )(before, tiles, *xs, features, cotangent)


def run_place(pieces, factor, width):
    return pl.pallas_call(
        lambda *refs: place(factor, *refs),
        grid=(1,),
        in_specs=[whole(v.shape) for v in pieces],
        out_specs=[whole((width, width))] * 2,
        out_shape=[jax.ShapeDtypeStruct((width, width), F32)] * 2,
        compiler_params=params(24),
        cost_estimate=estimate(width * width, 16 * width * width),
        name="place",
    )(*pieces)


def run_finish(summed, cotangent, w_self, w_neigh):
    nodes, width = summed.shape
    return pl.pallas_call(
        finish,
        grid=(nodes // BLOCK,),
        in_specs=[row_spec(width), row_spec(width), whole(w_self.shape), whole(w_neigh.shape)],
        out_specs=row_spec(width),
        out_shape=jax.ShapeDtypeStruct((nodes, width), F32),
        compiler_params=params(24),
        cost_estimate=estimate(3 * nodes * width * width, 10 * nodes * width),
        name="finish",
    )(summed, cotangent, w_self, w_neigh)


BLK = ("z", "y", "core")


def moved(value, perm):
    return lax.ppermute(value, BLK, perm)


def turned(value, axis, by):
    length = lax.axis_size(axis)
    return lax.ppermute(value, axis, [(i, (i + by) % length) for i in range(length)])


def fence(values):
    return lax.optimization_barrier(values)


def on_device(
    features,
    cotangent,
    w_self,
    w_neigh,
    tile_src,
    tile_dst,
    tile_count,
    send_ids,
    recv_dst,
    recv_count,
):
    nodes, width = features.shape
    ngroup, cap = send_ids.shape[1], send_ids.shape[2]
    ept = tile_src.shape[2]
    nz, ny = lax.axis_size("z"), lax.axis_size("y")
    nblk = nz * ny * 2
    core, ypos = lax.axis_index("core"), lax.axis_index("y")
    ring = range(nblk)
    swap = [(0, 1), (1, 0)]

    def swapped(v):
        return lax.ppermute(v, "core", swap)

    x, rows, own, first, pair1, pair2, pair3 = run_whole(
        prepare,
        (tile_count, recv_count, tile_src, tile_dst, recv_dst, cotangent),
        [((nodes, width), BF16), ((ngroup, cap, width), BF16)]
        + [((1, ept), I32)] * 2
        + [((2, ept), I32)] * 3,
        ngroup * cap * nodes * width,
        "prepare",
    )
    far = turned(x, "z", -1)
    first = moved(first, [(i, (i - 1 if i % 2 else i - 7) % nblk) for i in ring])
    pairs = [
        moved(p, [(i, (i - 2 * j) % nblk) for i in ring])
        for j, p in ((1, pair1), (2, pair2), (3, pair3))
    ]
    rows = fence((rows, first))[0]
    returned = lax.all_to_all(rows, "group", split_axis=0, concat_axis=0, tiled=True)
    x, far = fence((x, far, first, pairs))[:2]

    one = turned(jnp.where(ypos == 0, far, x), "y", -1)
    three = turned(jnp.where(ypos == ny - 1, x, far), "y", 1)
    side = swapped(jnp.where(core == 1, x, far))
    other = swapped(jnp.concatenate([p[1:2] for p in pairs], axis=0))
    near = run_build(((own, 0), (first, 0)), nodes)
    quad = run_build(((pairs[0], 0), (pairs[2], 0), (other, 0), (other, 2)), nodes)
    mid = run_build(((pairs[1], 0), (other, 1)), nodes)
    one, three = fence((one, three, near, quad, mid, side))[:2]
    relay = jnp.where(core == 0, one, three)

    two = moved(
        relay,
        [(i, (i - 2 if i % 2 == 0 else i + 2) % nblk) for i in ring],
    )
    one_b = swapped(one)
    three_b = swapped(three)
    summed = run_most(
        near,
        quad,
        (x, side, one, three, one_b, three_b),
        send_ids.reshape(1, ngroup * cap),
        returned.reshape(ngroup * cap, width),
    )
    two = fence((two, summed))[0]

    two_b = swapped(two)
    summed, send, keep = run_last(
        summed, mid, (two, two_b), features, cotangent, ngroup * ny
    )

    part = keep + swapped(send)
    part = lax.all_to_all(part, ("group", "y"), split_axis=0, concat_axis=0, tiled=True).sum(0)

    def zflip(v, k):
        return lax.ppermute(v, "z", [(i, i ^ k) for i in range(nz)])

    part = part + zflip(part, 4)
    part, total = fence((part, run_finish(summed, cotangent, w_self, w_neigh)))
    part = (part + zflip(part, 1)) + (zflip(part, 2) + zflip(part, 3))
    part = jnp.stack([part] + [turned(part, "y", t) for t in range(1, ny)])
    held = [part] + [turned(part, "group", s) for s in range(1, ngroup)]
    held = held + [swapped(v) for v in held]
    factor = 1.0 / math.sqrt(nodes * ngroup * nblk)
    grad_self, grad_neigh = run_place(held, factor, width)
    return (total, grad_self, grad_neigh)


def solution(mesh):
    blk = mesh.shape["blk"]
    fine = Mesh(
        mesh.devices.reshape(mesh.shape["group"], blk // 8, 4, 2), ("group",) + BLK
    )
    both = ("group",) + BLK
    placed = (
        P(both, None),
        P(both, None),
        P(),
        P(),
        P(both, None, None),
        P(both, None, None),
        P(both, None),
        P(both, None, None),
        P(both, None, None),
        P(both, None),
    )
    return jax.shard_map(
        on_device,
        mesh=fine,
        in_specs=placed,
        out_specs=(P(both, None), P(), P()),
        check_vma=False,
    )
```

```python
import functools
import math

import jax
import jax.numpy as jnp
from jax import lax
from jax.experimental import pallas as pl
from jax.experimental.pallas import tpu as pltpu
from jax.sharding import Mesh
from jax.sharding import PartitionSpec as P

F32 = jnp.float32
BF16 = jnp.bfloat16
I32 = jnp.int32
CHUNK = 512
ALONG = (((1,), (1,)), ((), ()))
DOWN = (((0,), (0,)), ((), ()))


def dot(a, b, dims=(((1,), (0,)), ((), ()))):
    return lax.dot_general(a, b, dims, preferred_element_type=F32)


def hot(rows, ids):
    spots = lax.broadcasted_iota(I32, (rows, ids.shape[1]), 0)
    return jnp.where(spots == ids, 1.0, 0.0).astype(BF16)


def small_hot(rows, ids):
    spots = lax.broadcasted_iota(jnp.int16, (rows, ids.shape[1]), 0)
    ones = jnp.where(spots == ids.astype(jnp.int16), jnp.ones((), BF16), jnp.zeros((), BF16))
    return ones.astype(jnp.float8_e4m3fn)


def prepare(
    tcount, rcount, tsrc, tdst, rdst, cot, x_out, rows_out, own, beside, deep, pair1, pair2, pair3
):
    nodes = cot.shape[0]
    odd = lax.axis_index("core") == 1
    offs, ept = tdst.shape[1], tdst.shape[2]
    ngroup, cap = rdst.shape[1], rdst.shape[2]
    slot = lax.broadcasted_iota(I32, (1, ept), 1)
    counts = jnp.zeros((32, 32), F32)
    lists = []
    for s in range(offs):
        live = slot < tcount[0:1, s : s + 1]
        ids = jnp.where(live, tdst[0, s : s + 1, :], 1023)
        counts = counts + dot(hot(32, ids >> 5), hot(32, ids & 31), ALONG)
        lists.append(jnp.where(live, tsrc[0, s : s + 1, :] * 1024 + ids, -1))
    own[...] = lists[0]
    beside[...] = lists[1]
    deep[0:1, :] = lists[7]
    for j, pair in ((1, pair1), (2, pair2), (3, pair3)):
        pair[0:1, :] = lists[2 * j]
        pair[1:2, :] = jnp.where(odd, lists[2 * j + 1], lists[2 * j - 1])
    slot = lax.broadcasted_iota(I32, (1, cap), 1)
    marked = []
    for g in range(ngroup):
        ids = jnp.where(slot < rcount[0:1, g : g + 1], rdst[0, g : g + 1, :], 1023)
        counts = counts + dot(hot(32, ids >> 5), hot(32, ids & 31), ALONG)
        marked.append(hot(nodes, ids))
    upper = jnp.floor(counts * (1.0 / 128.0))
    lower = counts - upper * 128.0
    node = lax.broadcasted_iota(I32, (nodes, 32), 0)
    lane = lax.broadcasted_iota(I32, (nodes, 32), 1)
    pick = jnp.where((node >> 5) == lane, 1.0, 0.0).astype(BF16)
    spread = dot(pick, upper.astype(BF16)) * 128.0 + dot(pick, lower.astype(BF16))
    degree = jnp.sum(jnp.where((node & 31) == lane, spread, 0.0), axis=1, keepdims=True)
    inverse = 1.0 / jnp.maximum(degree, 1.0)
    along = jnp.transpose(jnp.broadcast_to(degree, (nodes, 128)))[0:1, :]
    deep[1:2, :] = jnp.zeros((1, ept), I32)
    deep[1:2, :nodes] = along.astype(I32)
    x = (inverse * cot[...].astype(F32)).astype(BF16)
    x_out[...] = x
    for g in range(ngroup):
        rows_out[g] = dot(marked[g], x, DOWN).astype(BF16)


def build(rows, *refs):
    lists, (tile_out, edges) = refs[:-2], refs[-2:]
    s = pl.program_id(0)
    nodes, ept = tile_out.shape[1], edges.shape[2]

    @pl.when(s == 0)
    def _():
        for k, row in enumerate(rows):
            edges[k] = lists[k][row : row + 1, :]

    live = jnp.sum((edges[s] >= 0).astype(I32))
    for low in range(0, ept, CHUNK):
        @pl.when((live <= low + CHUNK) & ((live > low) | (low == 0)))
        def _():
            packed = edges[s, :, : low + CHUNK]
            tile = dot(small_hot(nodes, packed >> 10), small_hot(nodes, packed & 1023), ALONG)
            tile_out[0] = tile.astype(BF16)


def most_sum(t0, t1, t2, t3, t4, t5, x0, x1, x2, x3, x4, x5, ids, rows, out):
    i = pl.program_id(0)
    block = out.shape[0]
    spots = lax.broadcasted_iota(I32, (block, ids.shape[1]), 0) + i * block
    total = dot(jnp.where(spots == ids[...], 1.0, 0.0).astype(BF16), rows[...])
    for tile, x in ((t0, x0), (t1, x1), (t2, x2), (t3, x3), (t4, x4), (t5, x5)):
        total = total + dot(tile[0], x[...])
    out[...] = total


def last_sum(before, tiles, x0, x1, feats, cot, out, send, keep, grad_self, grad_neigh):
    nodes = before.shape[0]
    grad_self[...] = dot(feats[...], cot[...], DOWN)
    for i in range(nodes // BLOCK):
        rows = slice(i * BLOCK, (i + 1) * BLOCK)
        total = before[rows, :] + dot(tiles[0, rows, :], x0[...])
        total = total + dot(tiles[1, rows, :], x1[...])
        out[rows, :] = total
        top = total.astype(BF16)
        rest = (total - top.astype(F32)).astype(BF16)
        part = dot(feats[rows, :], top, DOWN) + dot(feats[rows, :], rest, DOWN)
        if i == 0:
            grad_neigh[...] = part
        else:
            grad_neigh[...] += part
    pieces, _, size, _ = send.shape
    core = lax.axis_index("core")
    for n in range(pieces):
        here = pl.ds(pl.multiple_of((core * pieces + n) * size, size), size)
        there = pl.ds(pl.multiple_of(((1 - core) * pieces + n) * size, size), size)
        for m, grad in enumerate((grad_self, grad_neigh)):
            keep[n, m] = grad[here, :]
            send[n, m] = grad[there, :]


def place(factor, mine, theirs, out_self, out_neigh):
    pieces, _, size, _ = mine.shape
    core = lax.axis_index("core")
    for k, half in ((core, mine), (1 - core, theirs)):
        for n in range(pieces):
            at = pl.ds(pl.multiple_of((k * pieces + n) * size, size), size)
            out_self[at, :] = half[n, 0] * factor
            out_neigh[at, :] = half[n, 1] * factor


def finish(summed, cot, w_self, w_neigh, out):
    total = summed[...]
    top = total.astype(BF16)
    rest = (total - top.astype(F32)).astype(BF16)
    out[...] = (
        dot(cot[...], w_self[...], ALONG)
        + dot(top, w_neigh[...], ALONG)
        + dot(rest, w_neigh[...], ALONG)
    )


BLOCK = 256
MIB = 1024 * 1024


def params(mib):
    return pltpu.CompilerParams(vmem_limit_bytes=mib * MIB)


def whole(shape):
    return pl.BlockSpec(shape, lambda i: (0,) * len(shape))


def tile_spec(slot, nodes):
    return pl.BlockSpec((1, BLOCK, nodes), lambda i: (slot, i, 0))


def row_spec(width):
    return pl.BlockSpec((BLOCK, width), lambda i: (i, 0))


def estimate(macs, moved):
    return pl.CostEstimate(flops=2 * macs, bytes_accessed=moved, transcendentals=0)


def run_whole(kernel, given, made, macs, name):
    return pl.pallas_call(
        kernel,
        grid=(1,),
        out_shape=[jax.ShapeDtypeStruct(*m) for m in made],
        in_specs=[whole(v.shape) for v in given],
        out_specs=[whole(m[0]) for m in made],
        compiler_params=params(63),
        cost_estimate=estimate(macs, sum(2 * v.size for v in given)),
        name=name,
    )(*given)


def run_build(chosen, nodes):
    slots, ept = len(chosen), chosen[0][0].shape[1]
    rows = tuple(row for _, row in chosen)
    lists = [v for v, _ in chosen]
    return pl.pallas_call(
        functools.partial(build, rows),
        grid=(slots,),
        in_specs=[whole(v.shape) for v in lists],
        out_specs=pl.BlockSpec((1, nodes, nodes), lambda s: (s, 0, 0)),
        scratch_shapes=[pltpu.VMEM((slots, 1, ept), I32)],
        out_shape=jax.ShapeDtypeStruct((slots, nodes, nodes), BF16),
        compiler_params=params(60),
        cost_estimate=estimate(nodes * ept, nodes * ept),
        name="build",
    )(*lists)


def run_most(near, quad, xs, ids, rows):
    nodes, width = xs[0].shape
    return pl.pallas_call(
        most_sum,
        grid=(nodes // BLOCK,),
        in_specs=[tile_spec(s, nodes) for s in (0, 1, 0, 1, 2, 3)]
        + [whole(v.shape) for v in (*xs, ids, rows)],
        out_specs=row_spec(width),
        out_shape=jax.ShapeDtypeStruct((nodes, width), F32),
        compiler_params=params(56),
        cost_estimate=estimate(7 * nodes * nodes * width, 16 * nodes * width),
        name="most_sum",
    )(near, near, quad, quad, quad, quad, *xs, ids, rows)


def run_last(before, tiles, xs, features, cotangent, pieces):
    nodes, width = before.shape
    vm = pl.BlockSpec(memory_space=pltpu.VMEM)
    half = jax.ShapeDtypeStruct((pieces, 2, width // (2 * pieces), width), F32)
    return pl.pallas_call(
        last_sum,
        in_specs=[vm] * 6,
        out_specs=[vm] * 3,
        out_shape=(jax.ShapeDtypeStruct((nodes, width), F32), half, half),
        scratch_shapes=[pltpu.VMEM((width, width), F32)] * 2,
        compiler_params=params(24),
        cost_estimate=estimate(3 * nodes * nodes * width, 16 * nodes * width),
        name="last_sum",
    )(before, tiles, *xs, features, cotangent)


def run_place(pieces, factor, width):
    return pl.pallas_call(
        functools.partial(place, factor),
        grid=(1,),
        in_specs=[whole(v.shape) for v in pieces],
        out_specs=[whole((width, width))] * 2,
        out_shape=[jax.ShapeDtypeStruct((width, width), F32)] * 2,
        compiler_params=params(24),
        cost_estimate=estimate(width * width, 16 * width * width),
        name="place",
    )(*pieces)


def run_finish(summed, cotangent, w_self, w_neigh):
    nodes, width = summed.shape
    return pl.pallas_call(
        finish,
        grid=(nodes // BLOCK,),
        in_specs=[row_spec(width), row_spec(width), whole(w_self.shape), whole(w_neigh.shape)],
        out_specs=row_spec(width),
        out_shape=jax.ShapeDtypeStruct((nodes, width), F32),
        compiler_params=params(24),
        cost_estimate=estimate(3 * nodes * width * width, 10 * nodes * width),
        name="finish",
    )(summed, cotangent, w_self, w_neigh)


BLK = ("z", "y", "core")


def moved(value, perm):
    return lax.ppermute(value, BLK, perm)


def turned(value, axis, by):
    length = lax.axis_size(axis)
    return lax.ppermute(value, axis, [(i, (i + by) % length) for i in range(length)])


def fence(values):
    return lax.optimization_barrier(values)


def on_device(
    features,
    cotangent,
    w_self,
    w_neigh,
    tile_src,
    tile_dst,
    tile_count,
    send_ids,
    recv_dst,
    recv_count,
):
    nodes, width = features.shape
    ngroup, cap = send_ids.shape[1], send_ids.shape[2]
    ept = tile_src.shape[2]
    nz, ny = lax.axis_size("z"), lax.axis_size("y")
    nblk = nz * ny * 2
    core, ypos = lax.axis_index("core"), lax.axis_index("y")
    ring = range(nblk)
    swap = [(0, 1), (1, 0)]

    def swapped(v):
        return lax.ppermute(v, "core", swap)

    far = turned(cotangent, "z", -1)
    x, rows, own, beside, deep, pair1, pair2, pair3 = run_whole(
        prepare,
        (tile_count, recv_count, tile_src, tile_dst, recv_dst, cotangent),
        [((nodes, width), BF16), ((ngroup, cap, width), BF16)]
        + [((1, ept), I32)] * 2
        + [((2, ept), I32)] * 4,
        ngroup * cap * nodes * width,
        "prepare",
    )
    deep = turned(deep, "z", -1)
    pairs = [
        moved(p, [(i, (i - 2 * j) % nblk) for i in ring])
        for j, p in ((1, pair1), (2, pair2), (3, pair3))
    ]
    returned = lax.all_to_all(rows, "group", split_axis=0, concat_axis=0, tiled=True)
    x, far, deep, pairs = fence((x, far, deep, pairs))
    degree = deep[1, :nodes].astype(F32)
    inverse = 1.0 / jnp.maximum(degree, 1.0)
    far = (inverse[:, None] * far.astype(F32)).astype(BF16)

    one = turned(jnp.where(ypos == 0, far, x), "y", -1)
    three = turned(jnp.where(ypos == ny - 1, x, far), "y", 1)
    side = swapped(jnp.where(core == 1, x, far))
    beside = jnp.where(core == 1, beside, deep[0:1])
    other = swapped(jnp.concatenate([p[1:2] for p in pairs] + [beside], axis=0))
    near = run_build(((own, 0), (other, 3)), nodes)
    quad = run_build(((pairs[0], 0), (pairs[2], 0), (other, 0), (other, 2)), nodes)
    mid = run_build(((pairs[1], 0), (other, 1)), nodes)
    one, three = fence((one, three, near, quad, mid, side))[:2]
    relay = jnp.where(core == 0, one, three)

    two = moved(
        relay,
        [(i, (i - 2 if i % 2 == 0 else i + 2) % nblk) for i in ring],
    )
    one_b = swapped(one)
    three_b = swapped(three)
    summed = run_most(
        near,
        quad,
        (x, side, one, three, one_b, three_b),
        send_ids.reshape(1, ngroup * cap),
        returned.reshape(ngroup * cap, width),
    )
    two = fence((two, summed))[0]

    two_b = swapped(two)
    summed, send, keep = run_last(
        summed, mid, (two, two_b), features, cotangent, ngroup * ny
    )

    part = keep + swapped(send)
    part = lax.all_to_all(part, ("group", "y"), split_axis=0, concat_axis=0, tiled=True).sum(0)

    def zflip(v, k):
        return lax.ppermute(v, "z", [(i, i ^ k) for i in range(nz)])

    part = part + zflip(part, 4)
    part, total = fence((part, run_finish(summed, cotangent, w_self, w_neigh)))
    part = (part + zflip(part, 1)) + (zflip(part, 2) + zflip(part, 3))
    part = jnp.broadcast_to(part[None], (ngroup * ny,) + part.shape)
    part = lax.all_to_all(part, ("group", "y"), split_axis=0, concat_axis=0, tiled=True)
    held = (part, swapped(part))
    factor = 1.0 / math.sqrt(nodes * ngroup * nblk)
    grad_self, grad_neigh = run_place(held, factor, width)
    return (total, grad_self, grad_neigh)


def solution(mesh):
    blk = mesh.shape["blk"]
    fine = Mesh(
        mesh.devices.reshape(mesh.shape["group"], blk // 8, 4, 2), ("group",) + BLK
    )
    both = ("group",) + BLK
    placed = (
        P(both, None),
        P(both, None),
        P(),
        P(),
        P(both, None, None),
        P(both, None, None),
        P(both, None),
        P(both, None, None),
        P(both, None, None),
        P(both, None),
    )
    return jax.shard_map(
        on_device,
        mesh=fine,
        in_specs=placed,
        out_specs=(P(both, None), P(), P()),
        check_vma=False,
    )
```

```python
import functools
import math

import jax
import jax.numpy as jnp
from jax import lax
from jax.experimental import pallas as pl
from jax.experimental.pallas import tpu as pltpu
from jax.sharding import Mesh
from jax.sharding import PartitionSpec as P

F32 = jnp.float32
BF16 = jnp.bfloat16
I32 = jnp.int32
CHUNK = 512
ALONG = (((1,), (1,)), ((), ()))
DOWN = (((0,), (0,)), ((), ()))


def dot(a, b, dims=(((1,), (0,)), ((), ()))):
    return lax.dot_general(a, b, dims, preferred_element_type=F32)


def hot(rows, ids):
    spots = lax.broadcasted_iota(I32, (rows, ids.shape[1]), 0)
    return jnp.where(spots == ids, 1.0, 0.0).astype(BF16)


def small_hot(rows, ids):
    spots = lax.broadcasted_iota(jnp.int16, (rows, ids.shape[1]), 0)
    ones = jnp.where(spots == ids.astype(jnp.int16), jnp.ones((), BF16), jnp.zeros((), BF16))
    return ones.astype(jnp.float8_e4m3fn)


def prepare(
    tcount, rcount, tsrc, tdst, rdst, cot, x_out, rows_out, own, beside, deep, pair1, pair2, pair3
):
    nodes = cot.shape[0]
    odd = lax.axis_index("core") == 1
    offs, ept = tdst.shape[1], tdst.shape[2]
    ngroup, cap = rdst.shape[1], rdst.shape[2]
    slot = lax.broadcasted_iota(I32, (1, ept), 1)
    counts = jnp.zeros((32, 32), F32)
    lists = []
    for s in range(offs):
        live = slot < tcount[0:1, s : s + 1]
        ids = jnp.where(live, tdst[0, s : s + 1, :], 1023)
        counts = counts + dot(hot(32, ids >> 5), hot(32, ids & 31), ALONG)
        lists.append(jnp.where(live, tsrc[0, s : s + 1, :] * 1024 + ids, -1))
    own[...] = lists[0]
    beside[...] = lists[1]
    deep[0:1, :] = lists[7]
    for j, pair in ((1, pair1), (2, pair2), (3, pair3)):
        pair[0:1, :] = lists[2 * j]
        pair[1:2, :] = jnp.where(odd, lists[2 * j + 1], lists[2 * j - 1])
    slot = lax.broadcasted_iota(I32, (1, cap), 1)
    marked = []
    for g in range(ngroup):
        ids = jnp.where(slot < rcount[0:1, g : g + 1], rdst[0, g : g + 1, :], 1023)
        counts = counts + dot(hot(32, ids >> 5), hot(32, ids & 31), ALONG)
        marked.append(hot(nodes, ids))
    upper = jnp.floor(counts * (1.0 / 128.0))
    lower = counts - upper * 128.0
    node = lax.broadcasted_iota(I32, (nodes, 32), 0)
    lane = lax.broadcasted_iota(I32, (nodes, 32), 1)
    pick = jnp.where((node >> 5) == lane, 1.0, 0.0).astype(BF16)
    spread = dot(pick, upper.astype(BF16)) * 128.0 + dot(pick, lower.astype(BF16))
    degree = jnp.sum(jnp.where((node & 31) == lane, spread, 0.0), axis=1, keepdims=True)
    inverse = 1.0 / jnp.maximum(degree, 1.0)
    along = jnp.transpose(jnp.broadcast_to(degree, (nodes, 128)))[0:1, :]
    deep[1:2, :] = jnp.zeros((1, ept), I32)
    deep[1:2, :nodes] = along.astype(I32)
    x = (inverse * cot[...].astype(F32)).astype(BF16)
    x_out[...] = x
    for g in range(ngroup):
        rows_out[g] = dot(marked[g], x, DOWN).astype(BF16)


def build(rows, *refs):
    lists, (tile_out, edges) = refs[:-2], refs[-2:]
    s = pl.program_id(0)
    nodes, ept = tile_out.shape[1], edges.shape[2]

    @pl.when(s == 0)
    def _():
        for k, row in enumerate(rows):
            edges[k] = lists[k][row : row + 1, :]

    live = jnp.sum((edges[s] >= 0).astype(I32))
    for low in range(0, ept, CHUNK):
        @pl.when((live <= low + CHUNK) & ((live > low) | (low == 0)))
        def _():
            packed = edges[s, :, : low + CHUNK]
            tile = dot(small_hot(nodes, packed >> 10), small_hot(nodes, packed & 1023), ALONG)
            tile_out[0] = tile.astype(BF16)


def most_sum(t0, t1, t2, t3, t4, t5, x0, x1, x2, x3, x4, x5, ids, rows, out):
    i = pl.program_id(0)
    block = out.shape[0]
    spots = lax.broadcasted_iota(I32, (block, ids.shape[1]), 0) + i * block
    total = dot(jnp.where(spots == ids[...], 1.0, 0.0).astype(BF16), rows[...])
    for tile, x in ((t0, x0), (t1, x1), (t2, x2), (t3, x3), (t4, x4), (t5, x5)):
        total = total + dot(tile[0], x[...])
    out[...] = total


def choose(deep, x, far, one, three, side):
    i = pl.program_id(0)
    block = x.shape[0]
    degree = deep[1:2, pl.ds(pl.multiple_of(i * block, block), block)].astype(F32)
    column = jnp.transpose(jnp.broadcast_to(degree, (128, block)))[:, 0:1]
    scaled = ((1.0 / jnp.maximum(column, 1.0)) * far[...].astype(F32)).astype(BF16)
    near = x[...]
    y, core = lax.axis_index("y"), lax.axis_index("core")
    one[...] = jnp.where(y == 0, scaled, near)
    three[...] = jnp.where(y == lax.axis_size("y") - 1, near, scaled)
    side[...] = jnp.where(core == 1, near, scaled)


def relay(one, three, out):
    out[...] = jnp.where(lax.axis_index("core") == 0, one[...], three[...])


def last_sum(before, tiles, x0, x1, feats, cot, out, send, keep, grad_self, grad_neigh):
    nodes = before.shape[0]
    grad_self[...] = dot(feats[...], cot[...], DOWN)
    for i in range(nodes // BLOCK):
        rows = slice(i * BLOCK, (i + 1) * BLOCK)
        total = before[rows, :] + dot(tiles[0, rows, :], x0[...])
        total = total + dot(tiles[1, rows, :], x1[...])
        out[rows, :] = total
        top = total.astype(BF16)
        rest = (total - top.astype(F32)).astype(BF16)
        part = dot(feats[rows, :], top, DOWN) + dot(feats[rows, :], rest, DOWN)
        if i == 0:
            grad_neigh[...] = part
        else:
            grad_neigh[...] += part
    pieces, _, size, _ = send.shape
    core = lax.axis_index("core")
    for n in range(pieces):
        here = pl.ds(pl.multiple_of((core * pieces + n) * size, size), size)
        there = pl.ds(pl.multiple_of(((1 - core) * pieces + n) * size, size), size)
        for m, grad in enumerate((grad_self, grad_neigh)):
            keep[n, m] = grad[here, :]
            send[n, m] = grad[there, :]


def place(factor, mine, theirs, out_self, out_neigh):
    pieces, _, size, _ = mine.shape
    core = lax.axis_index("core")
    for k, half in ((core, mine), (1 - core, theirs)):
        for n in range(pieces):
            at = pl.ds(pl.multiple_of((k * pieces + n) * size, size), size)
            out_self[at, :] = half[n, 0].astype(F32) * factor
            out_neigh[at, :] = (half[n, 1].astype(F32) + half[n, 2].astype(F32)) * factor


def finish(summed, cot, w_self, w_neigh, out):
    total = summed[...]
    top = total.astype(BF16)
    rest = (total - top.astype(F32)).astype(BF16)
    out[...] = (
        dot(cot[...], w_self[...], ALONG)
        + dot(top, w_neigh[...], ALONG)
        + dot(rest, w_neigh[...], ALONG)
    )


BLOCK = 256
MIB = 1024 * 1024


def params(mib):
    return pltpu.CompilerParams(vmem_limit_bytes=mib * MIB)


def whole(shape):
    return pl.BlockSpec(shape, lambda i: (0,) * len(shape))


def tile_spec(slot, nodes):
    return pl.BlockSpec((1, BLOCK, nodes), lambda i: (slot, i, 0))


def row_spec(width):
    return pl.BlockSpec((BLOCK, width), lambda i: (i, 0))


def estimate(macs, moved):
    return pl.CostEstimate(flops=2 * macs, bytes_accessed=moved, transcendentals=0)


def run_whole(kernel, given, made, macs, name):
    return pl.pallas_call(
        kernel,
        grid=(1,),
        out_shape=[jax.ShapeDtypeStruct(*m) for m in made],
        in_specs=[whole(v.shape) for v in given],
        out_specs=[whole(m[0]) for m in made],
        compiler_params=params(63),
        cost_estimate=estimate(macs, sum(2 * v.size for v in given)),
        name=name,
    )(*given)


def run_build(chosen, nodes):
    slots, ept = len(chosen), chosen[0][0].shape[1]
    rows = tuple(row for _, row in chosen)
    lists = [v for v, _ in chosen]
    return pl.pallas_call(
        functools.partial(build, rows),
        grid=(slots,),
        in_specs=[whole(v.shape) for v in lists],
        out_specs=pl.BlockSpec((1, nodes, nodes), lambda s: (s, 0, 0)),
        scratch_shapes=[pltpu.VMEM((slots, 1, ept), I32)],
        out_shape=jax.ShapeDtypeStruct((slots, nodes, nodes), BF16),
        compiler_params=params(60),
        cost_estimate=estimate(nodes * ept, nodes * ept),
        name="build",
    )(*lists)


def run_most(near, quad, xs, ids, rows):
    nodes, width = xs[0].shape
    return pl.pallas_call(
        most_sum,
        grid=(nodes // BLOCK,),
        in_specs=[tile_spec(s, nodes) for s in (0, 1, 0, 1, 2, 3)]
        + [whole(v.shape) for v in (*xs, ids, rows)],
        out_specs=row_spec(width),
        out_shape=jax.ShapeDtypeStruct((nodes, width), F32),
        compiler_params=params(56),
        cost_estimate=estimate(7 * nodes * nodes * width, 16 * nodes * width),
        name="most_sum",
    )(near, near, quad, quad, quad, quad, *xs, ids, rows)


def run_rows(kernel, given, made, name):
    nodes, width = given[-1].shape
    lead = [whole(v.shape) for v in given if v.shape[0] != nodes]
    return pl.pallas_call(
        kernel,
        grid=(nodes // BLOCK,),
        in_specs=lead + [row_spec(width)] * (len(given) - len(lead)),
        out_specs=[row_spec(width)] * made,
        out_shape=[jax.ShapeDtypeStruct((nodes, width), BF16)] * made,
        compiler_params=params(64),
        cost_estimate=estimate(nodes * width, 2 * (made + 2) * nodes * width),
        name=name,
    )(*given)


def run_last(before, tiles, xs, features, cotangent, pieces):
    nodes, width = before.shape
    vm = pl.BlockSpec(memory_space=pltpu.VMEM)
    half = jax.ShapeDtypeStruct((pieces, 2, width // (2 * pieces), width), F32)
    return pl.pallas_call(
        last_sum,
        in_specs=[vm] * 6,
        out_specs=[vm] * 3,
        out_shape=(jax.ShapeDtypeStruct((nodes, width), F32), half, half),
        scratch_shapes=[pltpu.VMEM((width, width), F32)] * 2,
        compiler_params=params(24),
        cost_estimate=estimate(3 * nodes * nodes * width, 16 * nodes * width),
        name="last_sum",
    )(before, tiles, *xs, features, cotangent)


def run_place(pieces, factor, width):
    return pl.pallas_call(
        functools.partial(place, factor),
        grid=(1,),
        in_specs=[whole(v.shape) for v in pieces],
        out_specs=[whole((width, width))] * 2,
        out_shape=[jax.ShapeDtypeStruct((width, width), F32)] * 2,
        compiler_params=params(24),
        cost_estimate=estimate(width * width, 16 * width * width),
        name="place",
    )(*pieces)


def run_finish(summed, cotangent, w_self, w_neigh):
    nodes, width = summed.shape
    return pl.pallas_call(
        finish,
        grid=(nodes // BLOCK,),
        in_specs=[row_spec(width), row_spec(width), whole(w_self.shape), whole(w_neigh.shape)],
        out_specs=row_spec(width),
        out_shape=jax.ShapeDtypeStruct((nodes, width), F32),
        compiler_params=params(24),
        cost_estimate=estimate(3 * nodes * width * width, 10 * nodes * width),
        name="finish",
    )(summed, cotangent, w_self, w_neigh)


BLK = ("z", "y", "core")


def moved(value, perm):
    return lax.ppermute(value, BLK, perm)


def turned(value, axis, by):
    length = lax.axis_size(axis)
    return lax.ppermute(value, axis, [(i, (i + by) % length) for i in range(length)])


def fence(values):
    return lax.optimization_barrier(values)


def on_device(
    features,
    cotangent,
    w_self,
    w_neigh,
    tile_src,
    tile_dst,
    tile_count,
    send_ids,
    recv_dst,
    recv_count,
):
    nodes, width = features.shape
    ngroup, cap = send_ids.shape[1], send_ids.shape[2]
    ept = tile_src.shape[2]
    nz, ny = lax.axis_size("z"), lax.axis_size("y")
    nblk = nz * ny * 2
    core = lax.axis_index("core")
    ring = range(nblk)
    swap = [(0, 1), (1, 0)]

    def swapped(v):
        return lax.ppermute(v, "core", swap)

    far = turned(cotangent, "z", -1)
    x, rows, own, beside, deep, pair1, pair2, pair3 = run_whole(
        prepare,
        (tile_count, recv_count, tile_src, tile_dst, recv_dst, cotangent),
        [((nodes, width), BF16), ((ngroup, cap, width), BF16)]
        + [((1, ept), I32)] * 2
        + [((2, ept), I32)] * 4,
        ngroup * cap * nodes * width,
        "prepare",
    )
    deep = turned(deep, "z", -1)
    pairs = [
        moved(p, [(i, (i - 2 * j) % nblk) for i in ring])
        for j, p in ((1, pair1), (2, pair2), (3, pair3))
    ]
    returned = lax.all_to_all(rows, "group", split_axis=0, concat_axis=0, tiled=True)
    x, far, deep, pairs = fence((x, far, deep, pairs))

    one, three, side = run_rows(choose, (deep, x, far), 3, "choose")
    one = turned(one, "y", -1)
    three = turned(three, "y", 1)
    side = swapped(side)
    beside = jnp.where(core == 1, beside, deep[0:1])
    other = swapped(jnp.concatenate([p[1:2] for p in pairs] + [beside], axis=0))
    near = run_build(((own, 0), (other, 3)), nodes)
    quad = run_build(((pairs[0], 0), (pairs[2], 0), (other, 0), (other, 2)), nodes)
    mid = run_build(((pairs[1], 0), (other, 1)), nodes)
    one, three = fence((one, three, near, quad, mid, side))[:2]

    (two,) = run_rows(relay, (one, three), 1, "relay")
    one, three, two = fence((one, three, two))
    two = moved(two, [(i, (i - 2 if i % 2 == 0 else i + 2) % nblk) for i in ring])
    one_b = swapped(one)
    three_b = swapped(three)
    summed = run_most(
        near,
        quad,
        (x, side, one, three, one_b, three_b),
        send_ids.reshape(1, ngroup * cap),
        returned.reshape(ngroup * cap, width),
    )
    two = fence((two, summed))[0]

    two_b = swapped(two)
    summed, send, keep = run_last(
        summed, mid, (two, two_b), features, cotangent, ngroup * ny
    )

    part = keep + swapped(send)
    part = lax.all_to_all(part, ("group", "y"), split_axis=0, concat_axis=0, tiled=True).sum(0)

    def zflip(v, k):
        return lax.ppermute(v, "z", [(i, i ^ k) for i in range(nz)])

    part = part + zflip(part, 4)
    part, total = fence((part, run_finish(summed, cotangent, w_self, w_neigh)))
    part = (part + zflip(part, 1)) + (zflip(part, 2) + zflip(part, 3))
    top = part[1].astype(BF16)
    part = jnp.stack([part[0].astype(BF16), top, (part[1] - top.astype(F32)).astype(BF16)])
    part = jnp.broadcast_to(part[None], (ngroup * ny,) + part.shape)
    part = lax.all_to_all(part, ("group", "y"), split_axis=0, concat_axis=0, tiled=True)
    held = (part, swapped(part))
    factor = 1.0 / math.sqrt(nodes * ngroup * nblk)
    grad_self, grad_neigh = run_place(held, factor, width)
    return (total, grad_self, grad_neigh)


def solution(mesh):
    blk = mesh.shape["blk"]
    fine = Mesh(
        mesh.devices.reshape(mesh.shape["group"], blk // 8, 4, 2), ("group",) + BLK
    )
    both = ("group",) + BLK
    placed = (
        P(both, None),
        P(both, None),
        P(),
        P(),
        P(both, None, None),
        P(both, None, None),
        P(both, None),
        P(both, None, None),
        P(both, None, None),
        P(both, None),
    )
    return jax.shard_map(
        on_device,
        mesh=fine,
        in_specs=placed,
        out_specs=(P(both, None), P(), P()),
        check_vma=False,
    )
```

```python
import functools
import math

import jax
import jax.numpy as jnp
from jax import lax
from jax.experimental import pallas as pl
from jax.experimental.pallas import tpu as pltpu
from jax.sharding import Mesh
from jax.sharding import PartitionSpec as P

F32 = jnp.float32
BF16 = jnp.bfloat16
I32 = jnp.int32
CHUNK = 512
ALONG = (((1,), (1,)), ((), ()))
DOWN = (((0,), (0,)), ((), ()))


def dot(a, b, dims=(((1,), (0,)), ((), ()))):
    return lax.dot_general(a, b, dims, preferred_element_type=F32)


def hot(rows, ids):
    spots = lax.broadcasted_iota(I32, (rows, ids.shape[1]), 0)
    return jnp.where(spots == ids, 1.0, 0.0).astype(BF16)


def small_hot(rows, ids):
    spots = lax.broadcasted_iota(jnp.int16, (rows, ids.shape[1]), 0)
    ones = jnp.where(spots == ids.astype(jnp.int16), jnp.ones((), BF16), jnp.zeros((), BF16))
    return ones.astype(jnp.float8_e4m3fn)


def prepare(
    tcount, rcount, tsrc, tdst, rdst, cot, x_out, rows_out, own, beside, deep, pair1, pair2, pair3
):
    nodes = cot.shape[0]
    odd = lax.axis_index("core") == 1
    offs, ept = tdst.shape[1], tdst.shape[2]
    ngroup, cap = rdst.shape[1], rdst.shape[2]
    slot = lax.broadcasted_iota(I32, (1, ept), 1)
    counts = jnp.zeros((32, 32), F32)
    lists = []
    for s in range(offs):
        live = slot < tcount[0:1, s : s + 1]
        ids = jnp.where(live, tdst[0, s : s + 1, :], 1023)
        counts = counts + dot(hot(32, ids >> 5), hot(32, ids & 31), ALONG)
        lists.append(jnp.where(live, tsrc[0, s : s + 1, :] * 1024 + ids, -1))
    own[...] = lists[0]
    beside[...] = lists[1]
    deep[0:1, :] = lists[7]
    for j, pair in ((1, pair1), (2, pair2), (3, pair3)):
        pair[0:1, :] = lists[2 * j]
        pair[1:2, :] = jnp.where(odd, lists[2 * j + 1], lists[2 * j - 1])
    slot = lax.broadcasted_iota(I32, (1, cap), 1)
    marked = []
    for g in range(ngroup):
        ids = jnp.where(slot < rcount[0:1, g : g + 1], rdst[0, g : g + 1, :], 1023)
        counts = counts + dot(hot(32, ids >> 5), hot(32, ids & 31), ALONG)
        marked.append(hot(nodes, ids))
    upper = jnp.floor(counts * (1.0 / 128.0))
    lower = counts - upper * 128.0
    node = lax.broadcasted_iota(I32, (nodes, 32), 0)
    lane = lax.broadcasted_iota(I32, (nodes, 32), 1)
    pick = jnp.where((node >> 5) == lane, 1.0, 0.0).astype(BF16)
    spread = dot(pick, upper.astype(BF16)) * 128.0 + dot(pick, lower.astype(BF16))
    degree = jnp.sum(jnp.where((node & 31) == lane, spread, 0.0), axis=1, keepdims=True)
    inverse = 1.0 / jnp.maximum(degree, 1.0)
    along = jnp.transpose(jnp.broadcast_to(degree, (nodes, 128)))[0:1, :]
    deep[1:2, :] = jnp.zeros((1, ept), I32)
    deep[1:2, :nodes] = along.astype(I32)
    x = (inverse * cot[...].astype(F32)).astype(BF16)
    x_out[...] = x
    for g in range(ngroup):
        rows_out[g] = dot(marked[g], x, DOWN).astype(BF16)


def build(rows, *refs):
    lists, (tile_out, edges) = refs[:-2], refs[-2:]
    s = pl.program_id(0)
    nodes, ept = tile_out.shape[1], edges.shape[2]

    @pl.when(s == 0)
    def _():
        for k, row in enumerate(rows):
            edges[k] = lists[k][row : row + 1, :]

    live = jnp.sum((edges[s] >= 0).astype(I32))
    for low in range(0, ept, CHUNK):
        @pl.when((live <= low + CHUNK) & ((live > low) | (low == 0)))
        def _():
            packed = edges[s, :, : low + CHUNK]
            tile = dot(small_hot(nodes, packed >> 10), small_hot(nodes, packed & 1023), ALONG)
            tile_out[0] = tile.astype(BF16)


def most_sum(t0, t1, t2, t3, t4, t5, x0, x1, x2, x3, x4, x5, ids, rows, out):
    i = pl.program_id(0)
    block = out.shape[0]
    spots = lax.broadcasted_iota(I32, (block, ids.shape[1]), 0) + i * block
    total = dot(jnp.where(spots == ids[...], 1.0, 0.0).astype(BF16), rows[...])
    for tile, x in ((t0, x0), (t1, x1), (t2, x2), (t3, x3), (t4, x4), (t5, x5)):
        total = total + dot(tile[0], x[...])
    out[...] = total


def last_sum(before, tiles, x0, x1, feats, cot, out, send, keep, grad_self, grad_neigh):
    nodes = before.shape[0]
    grad_self[...] = dot(feats[...], cot[...], DOWN)
    for i in range(nodes // BLOCK):
        rows = slice(i * BLOCK, (i + 1) * BLOCK)
        total = before[rows, :] + dot(tiles[0, rows, :], x0[...])
        total = total + dot(tiles[1, rows, :], x1[...])
        out[rows, :] = total
        top = total.astype(BF16)
        rest = (total - top.astype(F32)).astype(BF16)
        part = dot(feats[rows, :], top, DOWN) + dot(feats[rows, :], rest, DOWN)
        if i == 0:
            grad_neigh[...] = part
        else:
            grad_neigh[...] += part
    pieces, _, size, _ = send.shape
    core = lax.axis_index("core")
    for n in range(pieces):
        here = pl.ds(pl.multiple_of((core * pieces + n) * size, size), size)
        there = pl.ds(pl.multiple_of(((1 - core) * pieces + n) * size, size), size)
        for m, grad in enumerate((grad_self, grad_neigh)):
            keep[n, m] = grad[here, :]
            send[n, m] = grad[there, :]


def place(factor, mine, theirs, out_self, out_neigh):
    pieces, _, size, _ = mine.shape
    core = lax.axis_index("core")
    for k, half in ((core, mine), (1 - core, theirs)):
        for n in range(pieces):
            at = pl.ds(pl.multiple_of((k * pieces + n) * size, size), size)
            out_self[at, :] = half[n, 0].astype(F32) * factor
            out_neigh[at, :] = (half[n, 1].astype(F32) + half[n, 2].astype(F32)) * factor


def finish(summed, cot, w_self, w_neigh, out):
    total = summed[...]
    top = total.astype(BF16)
    rest = (total - top.astype(F32)).astype(BF16)
    out[...] = (
        dot(cot[...], w_self[...], ALONG)
        + dot(top, w_neigh[...], ALONG)
        + dot(rest, w_neigh[...], ALONG)
    )


BLOCK = 256
MIB = 1024 * 1024


def params(mib):
    return pltpu.CompilerParams(vmem_limit_bytes=mib * MIB)


def whole(shape):
    return pl.BlockSpec(shape, lambda i: (0,) * len(shape))


def tile_spec(slot, nodes):
    return pl.BlockSpec((1, BLOCK, nodes), lambda i: (slot, i, 0))


def row_spec(width):
    return pl.BlockSpec((BLOCK, width), lambda i: (i, 0))


def estimate(macs, moved):
    return pl.CostEstimate(flops=2 * macs, bytes_accessed=moved, transcendentals=0)


def run_whole(kernel, given, made, macs, name):
    return pl.pallas_call(
        kernel,
        grid=(1,),
        out_shape=[jax.ShapeDtypeStruct(*m) for m in made],
        in_specs=[whole(v.shape) for v in given],
        out_specs=[whole(m[0]) for m in made],
        compiler_params=params(63),
        cost_estimate=estimate(macs, sum(2 * v.size for v in given)),
        name=name,
    )(*given)


def run_build(chosen, nodes):
    slots, ept = len(chosen), chosen[0][0].shape[1]
    rows = tuple(row for _, row in chosen)
    lists = [v for v, _ in chosen]
    return pl.pallas_call(
        functools.partial(build, rows),
        grid=(slots,),
        in_specs=[whole(v.shape) for v in lists],
        out_specs=pl.BlockSpec((1, nodes, nodes), lambda s: (s, 0, 0)),
        scratch_shapes=[pltpu.VMEM((slots, 1, ept), I32)],
        out_shape=jax.ShapeDtypeStruct((slots, nodes, nodes), BF16),
        compiler_params=params(60),
        cost_estimate=estimate(nodes * ept, nodes * ept),
        name="build",
    )(*lists)


def run_most(near, quad, xs, ids, rows):
    nodes, width = xs[0].shape
    return pl.pallas_call(
        most_sum,
        grid=(nodes // BLOCK,),
        in_specs=[tile_spec(s, nodes) for s in (0, 1, 0, 1, 2, 3)]
        + [whole(v.shape) for v in (*xs, ids, rows)],
        out_specs=row_spec(width),
        out_shape=jax.ShapeDtypeStruct((nodes, width), F32),
        compiler_params=params(56),
        cost_estimate=estimate(7 * nodes * nodes * width, 16 * nodes * width),
        name="most_sum",
    )(near, near, quad, quad, quad, quad, *xs, ids, rows)


def run_last(before, tiles, xs, features, cotangent, pieces):
    nodes, width = before.shape
    vm = pl.BlockSpec(memory_space=pltpu.VMEM)
    half = jax.ShapeDtypeStruct((pieces, 2, width // (2 * pieces), width), F32)
    return pl.pallas_call(
        last_sum,
        in_specs=[vm] * 6,
        out_specs=[vm] * 3,
        out_shape=(jax.ShapeDtypeStruct((nodes, width), F32), half, half),
        scratch_shapes=[pltpu.VMEM((width, width), F32)] * 2,
        compiler_params=params(24),
        cost_estimate=estimate(3 * nodes * nodes * width, 16 * nodes * width),
        name="last_sum",
    )(before, tiles, *xs, features, cotangent)


def run_place(pieces, factor, width):
    return pl.pallas_call(
        functools.partial(place, factor),
        grid=(1,),
        in_specs=[whole(v.shape) for v in pieces],
        out_specs=[whole((width, width))] * 2,
        out_shape=[jax.ShapeDtypeStruct((width, width), F32)] * 2,
        compiler_params=params(24),
        cost_estimate=estimate(width * width, 16 * width * width),
        name="place",
    )(*pieces)


def run_finish(summed, cotangent, w_self, w_neigh):
    nodes, width = summed.shape
    return pl.pallas_call(
        finish,
        grid=(nodes // BLOCK,),
        in_specs=[row_spec(width), row_spec(width), whole(w_self.shape), whole(w_neigh.shape)],
        out_specs=row_spec(width),
        out_shape=jax.ShapeDtypeStruct((nodes, width), F32),
        compiler_params=params(24),
        cost_estimate=estimate(3 * nodes * width * width, 10 * nodes * width),
        name="finish",
    )(summed, cotangent, w_self, w_neigh)


BLK = ("z", "y", "core")


def moved(value, perm):
    return lax.ppermute(value, BLK, perm)


def turned(value, axis, by):
    length = lax.axis_size(axis)
    return lax.ppermute(value, axis, [(i, (i + by) % length) for i in range(length)])


def fence(values):
    return lax.optimization_barrier(values)


def on_device(
    features,
    cotangent,
    w_self,
    w_neigh,
    tile_src,
    tile_dst,
    tile_count,
    send_ids,
    recv_dst,
    recv_count,
):
    nodes, width = features.shape
    ngroup, cap = send_ids.shape[1], send_ids.shape[2]
    ept = tile_src.shape[2]
    nz, ny = lax.axis_size("z"), lax.axis_size("y")
    nblk = nz * ny * 2
    core, ypos = lax.axis_index("core"), lax.axis_index("y")
    ring = range(nblk)
    swap = [(0, 1), (1, 0)]

    def swapped(v):
        return lax.ppermute(v, "core", swap)

    far = turned(cotangent, "z", -1)
    x, rows, own, beside, deep, pair1, pair2, pair3 = run_whole(
        prepare,
        (tile_count, recv_count, tile_src, tile_dst, recv_dst, cotangent),
        [((nodes, width), BF16), ((ngroup, cap, width), BF16)]
        + [((1, ept), I32)] * 2
        + [((2, ept), I32)] * 4,
        ngroup * cap * nodes * width,
        "prepare",
    )
    deep = turned(deep, "z", -1)
    pairs = [
        moved(p, [(i, (i - 2 * j) % nblk) for i in ring])
        for j, p in ((1, pair1), (2, pair2), (3, pair3))
    ]
    returned = lax.all_to_all(rows, "group", split_axis=0, concat_axis=0, tiled=True)
    x, far, deep, pairs = fence((x, far, deep, pairs))
    degree = deep[1, :nodes].astype(F32)
    inverse = 1.0 / jnp.maximum(degree, 1.0)
    far = (inverse[:, None] * far.astype(F32)).astype(BF16)

    one = turned(jnp.where(ypos == 0, far, x), "y", -1)
    three = turned(jnp.where(ypos == ny - 1, x, far), "y", 1)
    side = swapped(jnp.where(core == 1, x, far))
    beside = jnp.where(core == 1, beside, deep[0:1])
    other = swapped(jnp.concatenate([p[1:2] for p in pairs] + [beside], axis=0))
    near = run_build(((own, 0), (other, 3)), nodes)
    quad = run_build(((pairs[0], 0), (pairs[2], 0), (other, 0), (other, 2)), nodes)
    mid = run_build(((pairs[1], 0), (other, 1)), nodes)
    one, three = fence((one, three, near, quad, mid, side))[:2]
    relay = jnp.where(core == 0, one, three)
    one, three, relay = fence((one, three, relay))

    two = moved(
        relay,
        [(i, (i - 2 if i % 2 == 0 else i + 2) % nblk) for i in ring],
    )
    one_b = swapped(one)
    three_b = swapped(three)
    summed = run_most(
        near,
        quad,
        (x, side, one, three, one_b, three_b),
        send_ids.reshape(1, ngroup * cap),
        returned.reshape(ngroup * cap, width),
    )
    two = fence((two, summed))[0]

    two_b = swapped(two)
    summed, send, keep = run_last(
        summed, mid, (two, two_b), features, cotangent, ngroup * ny
    )

    part = keep + swapped(send)
    part = lax.all_to_all(part, ("group", "y"), split_axis=0, concat_axis=0, tiled=True).sum(0)

    def zflip(v, k):
        return lax.ppermute(v, "z", [(i, i ^ k) for i in range(nz)])

    part = part + zflip(part, 4)
    part, total = fence((part, run_finish(summed, cotangent, w_self, w_neigh)))
    part = (part + zflip(part, 1)) + (zflip(part, 2) + zflip(part, 3))
    top = lax.reduce_precision(part[1], 8, 7)
    part = jnp.stack([part[0], top, part[1] - top]).astype(BF16)
    part = jnp.broadcast_to(part[None], (ngroup * ny,) + part.shape)
    part = lax.all_to_all(part, ("group", "y"), split_axis=0, concat_axis=0, tiled=True)
    held = (part, swapped(part))
    factor = 1.0 / math.sqrt(nodes * ngroup * nblk)
    grad_self, grad_neigh = run_place(held, factor, width)
    return (total, grad_self, grad_neigh)


def solution(mesh):
    blk = mesh.shape["blk"]
    fine = Mesh(
        mesh.devices.reshape(mesh.shape["group"], blk // 8, 4, 2), ("group",) + BLK
    )
    both = ("group",) + BLK
    placed = (
        P(both, None),
        P(both, None),
        P(),
        P(),
        P(both, None, None),
        P(both, None, None),
        P(both, None),
        P(both, None, None),
        P(both, None, None),
        P(both, None),
    )
    return jax.shard_map(
        on_device,
        mesh=fine,
        in_specs=placed,
        out_specs=(P(both, None), P(), P()),
        check_vma=False,
    )
```

```python
import functools
import math

import jax
import jax.numpy as jnp
from jax import lax
from jax.experimental import pallas as pl
from jax.experimental.pallas import tpu as pltpu
from jax.sharding import Mesh
from jax.sharding import PartitionSpec as P

F32 = jnp.float32
BF16 = jnp.bfloat16
I32 = jnp.int32
CHUNK = 512
ALONG = (((1,), (1,)), ((), ()))
DOWN = (((0,), (0,)), ((), ()))


def dot(a, b, dims=(((1,), (0,)), ((), ()))):
    return lax.dot_general(a, b, dims, preferred_element_type=F32)


def hot(rows, ids):
    spots = lax.broadcasted_iota(I32, (rows, ids.shape[1]), 0)
    return jnp.where(spots == ids, 1.0, 0.0).astype(BF16)


def small_hot(rows, ids):
    spots = lax.broadcasted_iota(jnp.int16, (rows, ids.shape[1]), 0)
    ones = jnp.where(spots == ids.astype(jnp.int16), jnp.ones((), BF16), jnp.zeros((), BF16))
    return ones.astype(jnp.float8_e4m3fn)


def prepare(
    tcount, rcount, tsrc, tdst, rdst, cot, x_out, rows_out, own, beside, deep, pair1, pair2, pair3
):
    nodes = cot.shape[0]
    odd = lax.axis_index("core") == 1
    offs, ept = tdst.shape[1], tdst.shape[2]
    ngroup, cap = rdst.shape[1], rdst.shape[2]
    slot = lax.broadcasted_iota(I32, (1, ept), 1)
    counts = jnp.zeros((32, 32), F32)
    lists = []
    for s in range(offs):
        live = slot < tcount[0:1, s : s + 1]
        ids = jnp.where(live, tdst[0, s : s + 1, :], 1023)
        counts = counts + dot(hot(32, ids >> 5), hot(32, ids & 31), ALONG)
        lists.append(jnp.where(live, tsrc[0, s : s + 1, :] * 1024 + ids, -1))
    own[...] = lists[0]
    beside[...] = lists[1]
    deep[0:1, :] = lists[7]
    for j, pair in ((1, pair1), (2, pair2), (3, pair3)):
        pair[0:1, :] = lists[2 * j]
        pair[1:2, :] = jnp.where(odd, lists[2 * j + 1], lists[2 * j - 1])
    slot = lax.broadcasted_iota(I32, (1, cap), 1)
    marked = []
    for g in range(ngroup):
        ids = jnp.where(slot < rcount[0:1, g : g + 1], rdst[0, g : g + 1, :], 1023)
        counts = counts + dot(hot(32, ids >> 5), hot(32, ids & 31), ALONG)
        marked.append(hot(nodes, ids))
    upper = jnp.floor(counts * (1.0 / 128.0))
    lower = counts - upper * 128.0
    node = lax.broadcasted_iota(I32, (nodes, 32), 0)
    lane = lax.broadcasted_iota(I32, (nodes, 32), 1)
    pick = jnp.where((node >> 5) == lane, 1.0, 0.0).astype(BF16)
    spread = dot(pick, upper.astype(BF16)) * 128.0 + dot(pick, lower.astype(BF16))
    degree = jnp.sum(jnp.where((node & 31) == lane, spread, 0.0), axis=1, keepdims=True)
    inverse = 1.0 / jnp.maximum(degree, 1.0)
    along = jnp.transpose(jnp.broadcast_to(degree, (nodes, 128)))[0:1, :]
    deep[1:2, :] = jnp.zeros((1, ept), I32)
    deep[1:2, :nodes] = along.astype(I32)
    x = (inverse * cot[...].astype(F32)).astype(BF16)
    x_out[...] = x
    for g in range(ngroup):
        rows_out[g] = dot(marked[g], x, DOWN).astype(BF16)


def build(rows, *refs):
    lists, (tile_out, edges) = refs[:-2], refs[-2:]
    s = pl.program_id(0)
    nodes, ept = tile_out.shape[1], edges.shape[2]

    @pl.when(s == 0)
    def _():
        for k, row in enumerate(rows):
            edges[k] = lists[k][row : row + 1, :]

    live = jnp.sum((edges[s] >= 0).astype(I32))

    @pl.when(live == 0)
    def _():
        tile_out[0] = jnp.zeros((nodes, nodes), BF16)

    for low in range(0, ept, CHUNK):
        @pl.when((live <= low + CHUNK) & (live > low))
        def _():
            packed = edges[s, :, : low + CHUNK]
            tile = dot(small_hot(nodes, packed >> 10), small_hot(nodes, packed & 1023), ALONG)
            tile_out[0] = tile.astype(BF16)


def most_sum(t0, t1, t2, t3, t4, t5, x0, x1, x2, x3, x4, x5, ids, rows, out):
    i = pl.program_id(0)
    block = out.shape[0]
    spots = lax.broadcasted_iota(I32, (block, ids.shape[1]), 0) + i * block
    total = dot(jnp.where(spots == ids[...], 1.0, 0.0).astype(BF16), rows[...])
    for tile, x in ((t0, x0), (t1, x1), (t2, x2), (t3, x3), (t4, x4), (t5, x5)):
        total = total + dot(tile[0], x[...])
    out[...] = total


def last_sum(before, tiles, x0, x1, feats, cot, out, send, keep, grad_self, grad_neigh):
    nodes = before.shape[0]
    grad_self[...] = dot(feats[...], cot[...], DOWN)
    for i in range(nodes // BLOCK):
        rows = slice(i * BLOCK, (i + 1) * BLOCK)
        total = before[rows, :] + dot(tiles[0, rows, :], x0[...])
        total = total + dot(tiles[1, rows, :], x1[...])
        out[rows, :] = total
        top = total.astype(BF16)
        rest = (total - top.astype(F32)).astype(BF16)
        part = dot(feats[rows, :], top, DOWN) + dot(feats[rows, :], rest, DOWN)
        if i == 0:
            grad_neigh[...] = part
        else:
            grad_neigh[...] += part
    pieces, _, size, _ = send.shape
    core = lax.axis_index("core")
    for n in range(pieces):
        here = pl.ds(pl.multiple_of((core * pieces + n) * size, size), size)
        there = pl.ds(pl.multiple_of(((1 - core) * pieces + n) * size, size), size)
        for m, grad in enumerate((grad_self, grad_neigh)):
            keep[n, m] = grad[here, :]
            send[n, m] = grad[there, :]


def place(factor, mine, theirs, out_self, out_neigh):
    pieces, _, size, _ = mine.shape
    core = lax.axis_index("core")
    for k, half in ((core, mine), (1 - core, theirs)):
        for n in range(pieces):
            at = pl.ds(pl.multiple_of((k * pieces + n) * size, size), size)
            out_self[at, :] = half[n, 0].astype(F32) * factor
            out_neigh[at, :] = (half[n, 1].astype(F32) + half[n, 2].astype(F32)) * factor


def finish(summed, cot, w_self, w_neigh, out):
    total = summed[...]
    top = total.astype(BF16)
    rest = (total - top.astype(F32)).astype(BF16)
    out[...] = (
        dot(cot[...], w_self[...], ALONG)
        + dot(top, w_neigh[...], ALONG)
        + dot(rest, w_neigh[...], ALONG)
    )


BLOCK = 256
MIB = 1024 * 1024


def params(mib):
    return pltpu.CompilerParams(vmem_limit_bytes=mib * MIB)


def whole(shape):
    return pl.BlockSpec(shape, lambda i: (0,) * len(shape))


def tile_spec(slot, nodes):
    return pl.BlockSpec((1, BLOCK, nodes), lambda i: (slot, i, 0))


def row_spec(width):
    return pl.BlockSpec((BLOCK, width), lambda i: (i, 0))


def estimate(macs, moved):
    return pl.CostEstimate(flops=2 * macs, bytes_accessed=moved, transcendentals=0)


def run_whole(kernel, given, made, macs, name):
    return pl.pallas_call(
        kernel,
        grid=(1,),
        out_shape=[jax.ShapeDtypeStruct(*m) for m in made],
        in_specs=[whole(v.shape) for v in given],
        out_specs=[whole(m[0]) for m in made],
        compiler_params=params(63),
        cost_estimate=estimate(macs, sum(2 * v.size for v in given)),
        name=name,
    )(*given)


def run_build(chosen, nodes):
    slots, ept = len(chosen), chosen[0][0].shape[1]
    rows = tuple(row for _, row in chosen)
    lists = [v for v, _ in chosen]
    return pl.pallas_call(
        functools.partial(build, rows),
        grid=(slots,),
        in_specs=[whole(v.shape) for v in lists],
        out_specs=pl.BlockSpec((1, nodes, nodes), lambda s: (s, 0, 0)),
        scratch_shapes=[pltpu.VMEM((slots, 1, ept), I32)],
        out_shape=jax.ShapeDtypeStruct((slots, nodes, nodes), BF16),
        compiler_params=params(60),
        cost_estimate=estimate(nodes * ept, nodes * ept),
        name="build",
    )(*lists)


def run_most(near, five, xs, ids, rows):
    nodes, width = xs[0].shape
    return pl.pallas_call(
        most_sum,
        grid=(nodes // BLOCK,),
        in_specs=[tile_spec(s, nodes) for s in (0, 0, 1, 2, 3, 4)]
        + [whole(v.shape) for v in (*xs, ids, rows)],
        out_specs=row_spec(width),
        out_shape=jax.ShapeDtypeStruct((nodes, width), F32),
        compiler_params=params(56),
        cost_estimate=estimate(7 * nodes * nodes * width, 16 * nodes * width),
        name="most_sum",
    )(near, *([five] * 5), *xs, ids, rows)


def run_last(before, tiles, xs, features, cotangent, pieces):
    nodes, width = before.shape
    vm = pl.BlockSpec(memory_space=pltpu.VMEM)
    half = jax.ShapeDtypeStruct((pieces, 2, width // (2 * pieces), width), F32)
    return pl.pallas_call(
        last_sum,
        in_specs=[vm] * 6,
        out_specs=[vm] * 3,
        out_shape=(jax.ShapeDtypeStruct((nodes, width), F32), half, half),
        scratch_shapes=[pltpu.VMEM((width, width), F32)] * 2,
        compiler_params=params(24),
        cost_estimate=estimate(3 * nodes * nodes * width, 16 * nodes * width),
        name="last_sum",
    )(before, tiles, *xs, features, cotangent)


def run_place(pieces, factor, width):
    return pl.pallas_call(
        functools.partial(place, factor),
        grid=(1,),
        in_specs=[whole(v.shape) for v in pieces],
        out_specs=[whole((width, width))] * 2,
        out_shape=[jax.ShapeDtypeStruct((width, width), F32)] * 2,
        compiler_params=params(24),
        cost_estimate=estimate(width * width, 16 * width * width),
        name="place",
    )(*pieces)


def run_finish(summed, cotangent, w_self, w_neigh):
    nodes, width = summed.shape
    return pl.pallas_call(
        finish,
        grid=(nodes // BLOCK,),
        in_specs=[row_spec(width), row_spec(width), whole(w_self.shape), whole(w_neigh.shape)],
        out_specs=row_spec(width),
        out_shape=jax.ShapeDtypeStruct((nodes, width), F32),
        compiler_params=params(24),
        cost_estimate=estimate(3 * nodes * width * width, 10 * nodes * width),
        name="finish",
    )(summed, cotangent, w_self, w_neigh)


BLK = ("z", "y", "core")


def moved(value, perm):
    return lax.ppermute(value, BLK, perm)


def turned(value, axis, by):
    length = lax.axis_size(axis)
    return lax.ppermute(value, axis, [(i, (i + by) % length) for i in range(length)])


def fence(values):
    return lax.optimization_barrier(values)


def on_device(
    features,
    cotangent,
    w_self,
    w_neigh,
    tile_src,
    tile_dst,
    tile_count,
    send_ids,
    recv_dst,
    recv_count,
):
    nodes, width = features.shape
    ngroup, cap = send_ids.shape[1], send_ids.shape[2]
    ept = tile_src.shape[2]
    nz, ny = lax.axis_size("z"), lax.axis_size("y")
    nblk = nz * ny * 2
    core, ypos = lax.axis_index("core"), lax.axis_index("y")
    ring = range(nblk)
    swap = [(0, 1), (1, 0)]

    def swapped(v):
        return lax.ppermute(v, "core", swap)

    far = turned(cotangent, "z", -1)
    x, rows, own, beside, deep, pair1, pair2, pair3 = run_whole(
        prepare,
        (tile_count, recv_count, tile_src, tile_dst, recv_dst, cotangent),
        [((nodes, width), BF16), ((ngroup, cap, width), BF16)]
        + [((1, ept), I32)] * 2
        + [((2, ept), I32)] * 4,
        ngroup * cap * nodes * width,
        "prepare",
    )
    deep = turned(deep, "z", -1)
    pairs = [
        moved(p, [(i, (i - 2 * j) % nblk) for i in ring])
        for j, p in ((1, pair1), (2, pair2), (3, pair3))
    ]
    returned = lax.all_to_all(rows, "group", split_axis=0, concat_axis=0, tiled=True)
    near = run_build(((own, 0),), nodes)
    x, far, deep, pairs = fence((x, far, deep, pairs, near))[:4]
    degree = deep[1, :nodes].astype(F32)
    inverse = 1.0 / jnp.maximum(degree, 1.0)
    far = (inverse[:, None] * far.astype(F32)).astype(BF16)

    one = turned(jnp.where(ypos == 0, far, x), "y", -1)
    three = turned(jnp.where(ypos == ny - 1, x, far), "y", 1)
    side = swapped(jnp.where(core == 1, x, far))
    beside = jnp.where(core == 1, beside, deep[0:1])
    other = swapped(jnp.concatenate([p[1:2] for p in pairs] + [beside], axis=0))
    five = run_build(
        ((other, 3), (pairs[0], 0), (pairs[2], 0), (other, 0), (other, 2)), nodes
    )
    mid = run_build(((pairs[1], 0), (other, 1)), nodes)
    one, three = fence((one, three, five, mid, side))[:2]
    relay = jnp.where(core == 0, one, three)
    one, three, relay = fence((one, three, relay))

    two = moved(
        relay,
        [(i, (i - 2 if i % 2 == 0 else i + 2) % nblk) for i in ring],
    )
    one_b = swapped(one)
    three_b = swapped(three)
    summed = run_most(
        near,
        five,
        (x, side, one, three, one_b, three_b),
        send_ids.reshape(1, ngroup * cap),
        returned.reshape(ngroup * cap, width),
    )
    two = fence((two, summed))[0]

    two_b = swapped(two)
    summed, send, keep = run_last(
        summed, mid, (two, two_b), features, cotangent, ngroup * ny
    )

    part = keep + swapped(send)
    part = lax.all_to_all(part, ("group", "y"), split_axis=0, concat_axis=0, tiled=True).sum(0)

    def zflip(v, k):
        return lax.ppermute(v, "z", [(i, i ^ k) for i in range(nz)])

    part = part + zflip(part, 4)
    part, total = fence((part, run_finish(summed, cotangent, w_self, w_neigh)))
    part = (part + zflip(part, 1)) + (zflip(part, 2) + zflip(part, 3))
    top = lax.reduce_precision(part[1], 8, 7)
    part = jnp.stack([part[0], top, part[1] - top]).astype(BF16)
    part = jnp.broadcast_to(part[None], (ngroup * ny,) + part.shape)
    part = lax.all_to_all(part, ("group", "y"), split_axis=0, concat_axis=0, tiled=True)
    held = (part, swapped(part))
    factor = 1.0 / math.sqrt(nodes * ngroup * nblk)
    grad_self, grad_neigh = run_place(held, factor, width)
    return (total, grad_self, grad_neigh)


def solution(mesh):
    blk = mesh.shape["blk"]
    fine = Mesh(
        mesh.devices.reshape(mesh.shape["group"], blk // 8, 4, 2), ("group",) + BLK
    )
    both = ("group",) + BLK
    placed = (
        P(both, None),
        P(both, None),
        P(),
        P(),
        P(both, None, None),
        P(both, None, None),
        P(both, None),
        P(both, None, None),
        P(both, None, None),
        P(both, None),
    )
    return jax.shard_map(
        on_device,
        mesh=fine,
        in_specs=placed,
        out_specs=(P(both, None), P(), P()),
        check_vma=False,
    )
```

```python
import functools
import math

import jax
import jax.numpy as jnp
from jax import lax
from jax.experimental import pallas as pl
from jax.experimental.pallas import tpu as pltpu
from jax.sharding import Mesh
from jax.sharding import PartitionSpec as P

F32 = jnp.float32
BF16 = jnp.bfloat16
I32 = jnp.int32
CHUNK = 512
ALONG = (((1,), (1,)), ((), ()))
DOWN = (((0,), (0,)), ((), ()))


def dot(a, b, dims=(((1,), (0,)), ((), ()))):
    return lax.dot_general(a, b, dims, preferred_element_type=F32)


def hot(rows, ids):
    spots = lax.broadcasted_iota(I32, (rows, ids.shape[1]), 0)
    return jnp.where(spots == ids, 1.0, 0.0).astype(BF16)


def small_hot(rows, ids):
    spots = lax.broadcasted_iota(jnp.int16, (rows, ids.shape[1]), 0)
    ones = jnp.where(spots == ids.astype(jnp.int16), jnp.ones((), BF16), jnp.zeros((), BF16))
    return ones.astype(jnp.float8_e4m3fn)


def prepare(
    tcount, rcount, tsrc, tdst, rdst, cot, x_out, rows_out, own, beside, deep, pair1, pair2, pair3
):
    nodes = cot.shape[0]
    odd = lax.axis_index("core") == 1
    offs, ept = tdst.shape[1], tdst.shape[2]
    ngroup, cap = rdst.shape[1], rdst.shape[2]
    slot = lax.broadcasted_iota(I32, (1, ept), 1)
    counts = jnp.zeros((32, 32), F32)
    lists = []
    for s in range(offs):
        live = slot < tcount[0:1, s : s + 1]
        ids = jnp.where(live, tdst[0, s : s + 1, :], 1023)
        counts = counts + dot(hot(32, ids >> 5), hot(32, ids & 31), ALONG)
        lists.append(jnp.where(live, tsrc[0, s : s + 1, :] * 1024 + ids, -1))
    own[...] = lists[0]
    beside[...] = lists[1]
    deep[0:1, :] = lists[7]
    for j, pair in ((1, pair1), (2, pair2), (3, pair3)):
        pair[0:1, :] = lists[2 * j]
        pair[1:2, :] = jnp.where(odd, lists[2 * j + 1], lists[2 * j - 1])
    slot = lax.broadcasted_iota(I32, (1, cap), 1)
    marked = []
    for g in range(ngroup):
        ids = jnp.where(slot < rcount[0:1, g : g + 1], rdst[0, g : g + 1, :], 1023)
        counts = counts + dot(hot(32, ids >> 5), hot(32, ids & 31), ALONG)
        marked.append(hot(nodes, ids))
    upper = jnp.floor(counts * (1.0 / 128.0))
    lower = counts - upper * 128.0
    node = lax.broadcasted_iota(I32, (nodes, 32), 0)
    lane = lax.broadcasted_iota(I32, (nodes, 32), 1)
    pick = jnp.where((node >> 5) == lane, 1.0, 0.0).astype(BF16)
    spread = dot(pick, upper.astype(BF16)) * 128.0 + dot(pick, lower.astype(BF16))
    degree = jnp.sum(jnp.where((node & 31) == lane, spread, 0.0), axis=1, keepdims=True)
    inverse = 1.0 / jnp.maximum(degree, 1.0)
    along = jnp.transpose(jnp.broadcast_to(degree, (nodes, 128)))[0:1, :]
    deep[1:2, :] = jnp.zeros((1, ept), I32)
    deep[1:2, :nodes] = along.astype(I32)
    x = (inverse * cot[...].astype(F32)).astype(BF16)
    x_out[...] = x
    for g in range(ngroup):
        rows_out[g] = dot(marked[g], x, DOWN).astype(BF16)


def build(rows, *refs):
    lists, (tile_out, edges) = refs[:-2], refs[-2:]
    s = pl.program_id(0)
    nodes, ept = tile_out.shape[1], edges.shape[2]

    @pl.when(s == 0)
    def _():
        for k, row in enumerate(rows):
            edges[k] = lists[k][row : row + 1, :]

    live = jnp.sum((edges[s] >= 0).astype(I32))

    @pl.when(live == 0)
    def _():
        tile_out[0] = jnp.zeros((nodes, nodes), BF16)

    for low in range(0, ept, CHUNK):
        @pl.when((live <= low + CHUNK) & (live > low))
        def _():
            packed = edges[s, :, : low + CHUNK]
            tile = dot(small_hot(nodes, packed >> 10), small_hot(nodes, packed & 1023), ALONG)
            tile_out[0] = tile.astype(BF16)


def most_sum(t0, t1, t2, t3, t4, t5, x0, x1, x2, x3, x4, x5, ids, rows, out):
    i = pl.program_id(0)
    block = out.shape[0]
    spots = lax.broadcasted_iota(I32, (block, ids.shape[1]), 0) + i * block
    total = dot(jnp.where(spots == ids[...], 1.0, 0.0).astype(BF16), rows[...])
    for tile, x in ((t0, x0), (t1, x1), (t2, x2), (t3, x3), (t4, x4), (t5, x5)):
        total = total + dot(tile[0], x[...])
    out[...] = total


def last_sum(before, tiles, x0, x1, feats, cot, out, send, keep, grad_self, grad_neigh):
    nodes = before.shape[0]
    grad_self[...] = dot(feats[...], cot[...], DOWN)
    for i in range(nodes // BLOCK):
        rows = slice(i * BLOCK, (i + 1) * BLOCK)
        total = before[rows, :] + dot(tiles[0, rows, :], x0[...])
        total = total + dot(tiles[1, rows, :], x1[...])
        out[rows, :] = total
        top = total.astype(BF16)
        rest = (total - top.astype(F32)).astype(BF16)
        part = dot(feats[rows, :], top, DOWN) + dot(feats[rows, :], rest, DOWN)
        if i == 0:
            grad_neigh[...] = part
        else:
            grad_neigh[...] += part
    pieces, _, size, _ = send.shape
    core = lax.axis_index("core")
    for n in range(pieces):
        here = pl.ds(pl.multiple_of((core * pieces + n) * size, size), size)
        there = pl.ds(pl.multiple_of(((1 - core) * pieces + n) * size, size), size)
        for m, grad in enumerate((grad_self, grad_neigh)):
            keep[n, m] = grad[here, :]
            send[n, m] = grad[there, :]


def place(factor, mine, theirs, out_self, out_neigh):
    pieces, _, size, _ = mine.shape
    core = lax.axis_index("core")
    for k, half in ((core, mine), (1 - core, theirs)):
        for n in range(pieces):
            at = pl.ds(pl.multiple_of((k * pieces + n) * size, size), size)
            out_self[at, :] = half[n, 0].astype(F32) * factor
            out_neigh[at, :] = (half[n, 1].astype(F32) + half[n, 2].astype(F32)) * factor


def finish(summed, cot, w_self, w_neigh, out):
    total = summed[...]
    top = total.astype(BF16)
    rest = (total - top.astype(F32)).astype(BF16)
    out[...] = (
        dot(cot[...], w_self[...], ALONG)
        + dot(top, w_neigh[...], ALONG)
        + dot(rest, w_neigh[...], ALONG)
    )


BLOCK = 256
MIB = 1024 * 1024


def params(mib):
    return pltpu.CompilerParams(vmem_limit_bytes=mib * MIB)


def whole(shape):
    return pl.BlockSpec(shape, lambda i: (0,) * len(shape))


def tile_spec(slot, nodes):
    return pl.BlockSpec((1, BLOCK, nodes), lambda i: (slot, i, 0))


def row_spec(width):
    return pl.BlockSpec((BLOCK, width), lambda i: (i, 0))


def estimate(macs, moved):
    return pl.CostEstimate(flops=2 * macs, bytes_accessed=moved, transcendentals=0)


def run_whole(kernel, given, made, macs, name):
    return pl.pallas_call(
        kernel,
        grid=(1,),
        out_shape=[jax.ShapeDtypeStruct(*m) for m in made],
        in_specs=[whole(v.shape) for v in given],
        out_specs=[whole(m[0]) for m in made],
        compiler_params=params(63),
        cost_estimate=estimate(macs, sum(2 * v.size for v in given)),
        name=name,
    )(*given)


def run_build(chosen, nodes):
    slots, ept = len(chosen), chosen[0][0].shape[1]
    rows = tuple(row for _, row in chosen)
    lists = [v for v, _ in chosen]
    return pl.pallas_call(
        functools.partial(build, rows),
        grid=(slots,),
        in_specs=[whole(v.shape) for v in lists],
        out_specs=pl.BlockSpec((1, nodes, nodes), lambda s: (s, 0, 0)),
        scratch_shapes=[pltpu.VMEM((slots, 1, ept), I32)],
        out_shape=jax.ShapeDtypeStruct((slots, nodes, nodes), BF16),
        compiler_params=params(60),
        cost_estimate=estimate(nodes * ept, nodes * ept),
        name="build",
    )(*lists)


def run_most(near, five, xs, ids, rows):
    nodes, width = xs[0].shape
    return pl.pallas_call(
        most_sum,
        grid=(nodes // BLOCK,),
        in_specs=[tile_spec(s, nodes) for s in (0, 0, 1, 2, 3, 4)]
        + [whole(v.shape) for v in (*xs, ids, rows)],
        out_specs=row_spec(width),
        out_shape=jax.ShapeDtypeStruct((nodes, width), F32),
        compiler_params=params(60),
        cost_estimate=estimate(7 * nodes * nodes * width, 16 * nodes * width),
        name="most_sum",
    )(near, *([five] * 5), *xs, ids, rows)


def run_last(before, tiles, xs, features, cotangent, pieces):
    nodes, width = before.shape
    vm = pl.BlockSpec(memory_space=pltpu.VMEM)
    half = jax.ShapeDtypeStruct((pieces, 2, width // (2 * pieces), width), F32)
    return pl.pallas_call(
        last_sum,
        in_specs=[vm] * 6,
        out_specs=[vm] * 3,
        out_shape=(jax.ShapeDtypeStruct((nodes, width), F32), half, half),
        scratch_shapes=[pltpu.VMEM((width, width), F32)] * 2,
        compiler_params=params(24),
        cost_estimate=estimate(3 * nodes * nodes * width, 16 * nodes * width),
        name="last_sum",
    )(before, tiles, *xs, features, cotangent)


def run_place(pieces, factor, width):
    return pl.pallas_call(
        functools.partial(place, factor),
        grid=(1,),
        in_specs=[whole(v.shape) for v in pieces],
        out_specs=[whole((width, width))] * 2,
        out_shape=[jax.ShapeDtypeStruct((width, width), F32)] * 2,
        compiler_params=params(24),
        cost_estimate=estimate(width * width, 16 * width * width),
        name="place",
    )(*pieces)


def run_finish(summed, cotangent, w_self, w_neigh):
    nodes, width = summed.shape
    return pl.pallas_call(
        finish,
        grid=(nodes // BLOCK,),
        in_specs=[row_spec(width), row_spec(width), whole(w_self.shape), whole(w_neigh.shape)],
        out_specs=row_spec(width),
        out_shape=jax.ShapeDtypeStruct((nodes, width), F32),
        compiler_params=params(24),
        cost_estimate=estimate(3 * nodes * width * width, 10 * nodes * width),
        name="finish",
    )(summed, cotangent, w_self, w_neigh)


BLK = ("z", "y", "core")


def moved(value, perm):
    return lax.ppermute(value, BLK, perm)


def turned(value, axis, by):
    length = lax.axis_size(axis)
    return lax.ppermute(value, axis, [(i, (i + by) % length) for i in range(length)])


def fence(values):
    return lax.optimization_barrier(values)


def on_device(
    features,
    cotangent,
    w_self,
    w_neigh,
    tile_src,
    tile_dst,
    tile_count,
    send_ids,
    recv_dst,
    recv_count,
):
    nodes, width = features.shape
    ngroup, cap = send_ids.shape[1], send_ids.shape[2]
    ept = tile_src.shape[2]
    nz, ny = lax.axis_size("z"), lax.axis_size("y")
    nblk = nz * ny * 2
    core, ypos = lax.axis_index("core"), lax.axis_index("y")
    ring = range(nblk)
    swap = [(0, 1), (1, 0)]

    def swapped(v):
        return lax.ppermute(v, "core", swap)

    far = turned(cotangent, "z", -1)
    x, rows, own, beside, deep, pair1, pair2, pair3 = run_whole(
        prepare,
        (tile_count, recv_count, tile_src, tile_dst, recv_dst, cotangent),
        [((nodes, width), BF16), ((ngroup, cap, width), BF16)]
        + [((1, ept), I32)] * 2
        + [((2, ept), I32)] * 4,
        ngroup * cap * nodes * width,
        "prepare",
    )
    deep = turned(deep, "z", -1)
    pairs = [
        moved(p, [(i, (i - 2 * j) % nblk) for i in ring])
        for j, p in ((1, pair1), (2, pair2), (3, pair3))
    ]
    returned = lax.all_to_all(rows, "group", split_axis=0, concat_axis=0, tiled=True)
    near = run_build(((own, 0),), nodes)
    ids = send_ids.reshape(1, ngroup * cap)
    x, far, deep, pairs, ids = fence((x, far, deep, pairs, ids, near))[:5]
    degree = deep[1, :nodes].astype(F32)
    inverse = 1.0 / jnp.maximum(degree, 1.0)
    far = (inverse[:, None] * far.astype(F32)).astype(BF16)

    one = turned(jnp.where(ypos == 0, far, x), "y", -1)
    three = turned(jnp.where(ypos == ny - 1, x, far), "y", 1)
    side = swapped(jnp.where(core == 1, x, far))
    beside = jnp.where(core == 1, beside, deep[0:1])
    other = swapped(jnp.concatenate([p[1:2] for p in pairs] + [beside], axis=0))
    five = run_build(
        ((other, 3), (pairs[0], 0), (pairs[2], 0), (other, 0), (other, 2)), nodes
    )
    mid = run_build(((pairs[1], 0), (other, 1)), nodes)
    one, three = fence((one, three, five, mid, side))[:2]
    relay = jnp.where(core == 0, one, three)
    one, three, relay = fence((one, three, relay))

    two = moved(
        relay,
        [(i, (i - 2 if i % 2 == 0 else i + 2) % nblk) for i in ring],
    )
    one_b = swapped(one)
    three_b = swapped(three)
    summed = run_most(
        near,
        five,
        (x, side, one, three, one_b, three_b),
        ids,
        returned.reshape(ngroup * cap, width),
    )
    two = fence((two, summed))[0]

    two_b = swapped(two)
    summed, send, keep = run_last(
        summed, mid, (two, two_b), features, cotangent, ngroup * ny
    )

    part = keep + swapped(send)
    part = lax.all_to_all(part, ("group", "y"), split_axis=0, concat_axis=0, tiled=True).sum(0)

    def zflip(v, k):
        return lax.ppermute(v, "z", [(i, i ^ k) for i in range(nz)])

    part = part + zflip(part, 4)
    part, total = fence((part, run_finish(summed, cotangent, w_self, w_neigh)))
    part = (part + zflip(part, 1)) + (zflip(part, 2) + zflip(part, 3))
    top = lax.reduce_precision(part[1], 8, 7)
    part = jnp.stack([part[0], top, part[1] - top]).astype(BF16)
    part = jnp.broadcast_to(part[None], (ngroup * ny,) + part.shape)
    part = lax.all_to_all(part, ("group", "y"), split_axis=0, concat_axis=0, tiled=True)
    held = (part, swapped(part))
    factor = 1.0 / math.sqrt(nodes * ngroup * nblk)
    grad_self, grad_neigh = run_place(held, factor, width)
    return (total, grad_self, grad_neigh)


def solution(mesh):
    blk = mesh.shape["blk"]
    fine = Mesh(
        mesh.devices.reshape(mesh.shape["group"], blk // 8, 4, 2), ("group",) + BLK
    )
    both = ("group",) + BLK
    placed = (
        P(both, None),
        P(both, None),
        P(),
        P(),
        P(both, None, None),
        P(both, None, None),
        P(both, None),
        P(both, None, None),
        P(both, None, None),
        P(both, None),
    )
    return jax.shard_map(
        on_device,
        mesh=fine,
        in_specs=placed,
        out_specs=(P(both, None), P(), P()),
        check_vma=False,
    )
```
